256 devices in a mesh: grp: 4 (over x), attn: 2 (over core), exp: 32 (over z, y).
Axes of the slice: x: 4, y: 4, z: 8, core: 2. Of those that a mesh axis runs over, the one named last changes fastest.
Arguments:
- hidden_rows: bfloat16 [32, 64, 5120], P('exp', 'grp', 'attn'), may hold values from -6 to 6
- routes: int32 [32, 64, 6], P('exp'), may hold values from 0 to 31, all different within a row; in each aligned block of 64 rows (0 to 63, 64 to 127, ..., all dimensions but the last counted through in order) at most 16 rows name the same one
- route_gain: float32 [32, 64, 6], P('exp'), may hold values from 0.1 to 1
- gate_weight: bfloat16 [32, 1536, 5120], P('exp', 'grp', 'attn'), may hold values from -0.078125 to 0.078125
- up_weight: bfloat16 [32, 1536, 5120], P('exp', 'grp', 'attn'), may hold values from -0.078125 to 0.078125
- down_weight: bfloat16 [32, 1536, 5120], P('exp', 'grp', 'attn'), may hold values from -0.21875 to 0.21875
Outputs:
- layer_out: bfloat16 [32, 64, 5120], P('exp', 'grp', 'attn')
The draws below stay inside these ranges and needn't reach their ends.
Inputs may be any that keep to these rules, and one draw needn't show every extreme that they name: `routes`: each row names 6 different experts. Among the 64 rows of one line no expert is named more than 16 times, and in every draw some expert is named exactly 16 times by the rows of one line; every expert is named somewhere.
All inputs are finite; a program needn't handle non-finite values.
Results may differ from the reference program's by a relative error of at most 0.022.
Values may be sent and summed in bfloat16 or wider, within the bound.
A program may use at most 64 MiB of HBM per device.

```python
import math
import jax
import jax.numpy as jnp
import numpy as np
from jax import lax

D = 5120
FF = 1536
TOPK = 6
SLAB_ROWS = 64
LINES = 32
EXPERTS = 32
CAPS = 16
N_GRP = 4


def spiked(array, stream_key, source, target, shards_of, factor):
    owner, partner = [(jnp.arange(array.shape[axis_at]) // (array.shape[axis_at] // shards_of)).reshape([-1 if axis == axis_at else 1 for axis in range(array.ndim)]) for axis_at in (source, target)]
    chosen = jax.random.permutation(stream_key, shards_of)[partner]
    strong = (owner == chosen) | (owner == (partner + shards_of // 2) % shards_of)
    return jnp.where(strong, factor * array, array)


def levels(key, shape, pieces, low, high):
    factor_of, own = 1.0, jax.random.fold_in(key, 6)
    for axis_at, blocks in pieces:
        steps = jnp.exp(jax.random.uniform(jax.random.fold_in(own, axis_at), (blocks,), jnp.float32, low / len(pieces), high / len(pieces)))
        factor_of = factor_of * jnp.repeat(steps, shape[axis_at] // blocks).reshape([-1 if axis == axis_at else 1 for axis in range(len(shape))])
    return factor_of


def routed_block(key, own, number, rows, amount, top, reach, lean):
    order = jax.random.permutation(key, amount)
    crowded, ordinary = load_shares(amount, rows * top, reach, lean, True), load_shares(amount, rows * top, reach, lean, False)
    places = jnp.arange(amount)

    def named(tallies, rotation):
        used = int((tallies > 0).sum())
        fixed = max(1, used // 4)
        moved = fixed + (places - fixed + rotation * (used - fixed)) % max(1, amount - fixed)
        return jnp.zeros((amount,), jnp.int32).at[order[jnp.where(places < fixed, places, moved)]].set(jnp.asarray(tallies, jnp.int32))

    tallies = jnp.where(number % 4 == 0, named(crowded, number // 4), named(ordinary, number - number // 4 - 1))
    mixed = jax.random.permutation(jax.random.fold_in(own, 3), amount)
    donor, sink = mixed[0:amount // 2 * 2:2], mixed[1:amount // 2 * 2:2]
    slack = jnp.minimum(tallies[donor] - 1, reach - tallies[sink]) // 2
    slack = jnp.where((donor == order[0]) | (sink == order[0]) | (tallies[sink] == 0), 0, jnp.maximum(slack, 0))
    moved = jax.random.randint(jax.random.fold_in(own, 4), (amount // 2,), 0, 1 << 20) % (slack + 1)
    tallies = tallies.at[donor].add(-moved).at[sink].add(moved)
    members = jnp.searchsorted(jnp.cumsum(tallies), jnp.arange(rows * top), side="right").astype(jnp.int32)
    table = members.reshape(top, rows).T
    table = table[jax.random.permutation(jax.random.fold_in(own, 1), rows)]
    rotation = jax.random.randint(jax.random.fold_in(own, 2), (rows, 1), 0, top)
    return jnp.take_along_axis(table, (jnp.arange(top)[None, :] + rotation) % top, axis=1)


def load_shares(count, total, most, lean, full):
    portions = [(1 << 20) // math.isqrt(standing ** lean) + 1 for standing in range(1, count + 1)]
    largest = most if full else min(most, max(-(-total // count), total * portions[0] // sum(portions)))
    least = 1 if total - largest >= count - 1 else 0
    holding, surplus = [largest] + [least] * (count - 1), total - largest - least * (count - 1)
    while surplus > 0:
        candidates = [i for i in range(1, count) if holding[i] < largest] or [i for i in range(1, count) if holding[i] < most]
        pool, left = sum([portions[i] for i in candidates]), surplus
        for i in candidates:
            more = min(most - holding[i], max(1, left * portions[i] // pool), surplus)
            holding[i] = holding[i] + more
            surplus = surplus - more
    return np.array(holding)


def centred(stream_key, extent, deviation, limit, split=(), held_as=jnp.bfloat16):
    gain = levels(stream_key, extent, split, -0.22, 0.18) if split else 1.0
    array = jax.random.normal(stream_key, extent, jnp.float32) * deviation * gain
    return jnp.minimum(jnp.maximum(array, -limit), limit).astype(held_as)


def heavy_noise(own_key, shape, scale, reach, pieces, heavy, held_as=jnp.bfloat16):
    entries = scale * jax.random.normal(own_key, shape, jnp.float32)
    if pieces:
        entries = entries * levels(own_key, shape, pieces, -0.22, 0.18)
    return jnp.clip(spiked(entries, jax.random.fold_in(own_key, 3), *heavy), -reach, reach).astype(held_as)


def setup_inputs(seed: int = 0) -> dict:
    seeds = jax.random.split(jax.random.key(seed), 7)
    hidden_rows = centred(seeds[0], (LINES, SLAB_ROWS, D), 1.0, 6.0, ((0, 32), (1, 4), (2, 2)))
    routes_keys = jax.random.split(jax.random.fold_in(seeds[1], 1), LINES * SLAB_ROWS // SLAB_ROWS)
    routes_turns = jax.random.permutation(jax.random.fold_in(seeds[1], 3), LINES * SLAB_ROWS // SLAB_ROWS)
    routes = jax.vmap(lambda own, number: routed_block(jax.random.fold_in(seeds[1], 2), own, number, SLAB_ROWS, EXPERTS, TOPK, CAPS, 2))(routes_keys, routes_turns).reshape((LINES, SLAB_ROWS, TOPK))
    route_gain = jnp.clip(jnp.exp(math.log(1.0) - 2.3025851 * jax.random.uniform(seeds[2], (LINES, SLAB_ROWS, TOPK), jnp.float32) ** levels(seeds[2], (LINES, SLAB_ROWS, TOPK), ((0, 32),), -0.2, 0.2)), 0.1, 1.0)
    gate_weight = centred(seeds[3], (EXPERTS, FF, D), D ** -0.5, 0.078125, ((0, 32), (1, 4), (2, 2)))
    up_weight = centred(seeds[4], (EXPERTS, FF, D), D ** -0.5, 0.078125, ((0, 32), (1, 4), (2, 2)))
    down_weight = heavy_noise(seeds[5], (EXPERTS, FF, D), FF ** -0.5, 0.21875, ((0, 32), (1, 4), (2, 2)), (1, 2, 4, 2.0))
    return dict(hidden_rows=hidden_rows, routes=routes, route_gain=route_gain, gate_weight=gate_weight, up_weight=up_weight, down_weight=down_weight)


def slot_tables(routes_line):
    slab = routes_line.shape[0]
    picks = (routes_line[:, :, None] == jnp.arange(EXPERTS, dtype=jnp.int32)[None, None, :]).astype(jnp.float32)
    counts = jnp.sum(picks, axis=1)
    lower = (jnp.arange(slab)[:, None] > jnp.arange(slab)[None, :]).astype(jnp.float32)
    before = jnp.dot(lower, counts, precision=lax.Precision.HIGHEST)
    grid = jnp.arange(CAPS).astype(jnp.float32)
    send = counts[:, :, None] * (before[:, :, None] == grid).astype(jnp.float32)
    send = jnp.transpose(send, (1, 2, 0))
    gather_tab = picks[:, :, :, None] * (before[:, None, :, None] == grid).astype(jnp.float32)
    return send, gather_tab.reshape(slab, picks.shape[1], EXPERTS * CAPS)


def reference(hidden_rows, routes, route_gain, gate_weight, up_weight, down_weight):
    sends, gathers = jax.vmap(slot_tables)(routes)
    rows_f = hidden_rows.astype(jnp.float32)
    block = FF // N_GRP
    dims = (((1,), (1,)), ((), ()))

    def one_expert(items):
        index, w_gate, w_up, w_down = items
        select = lax.dynamic_index_in_dim(sends, index, 1, keepdims=False)
        taken = jnp.einsum("lcs,lsd->lcd", select, rows_f).astype(jnp.bfloat16)
        flat = taken.reshape(-1, D)
        gate = lax.dot_general(flat, w_gate, dims, preferred_element_type=jnp.float32)
        upper = lax.dot_general(flat, w_up, dims, preferred_element_type=jnp.float32)
        act = (jax.nn.silu(gate) * upper).astype(jnp.bfloat16)
        act_b = act.astype(jnp.float32).reshape(-1, N_GRP, block)
        down_b = w_down.astype(jnp.float32).reshape(N_GRP, block, D)
        parts = jnp.einsum("mab,abd->mad", act_b, down_b).astype(jnp.bfloat16)
        parts = lax.optimization_barrier(parts)
        total = jnp.sum(parts.astype(jnp.float32), axis=1)
        return total.reshape(LINES, CAPS, D)

    outs = lax.map(one_expert, (jnp.arange(EXPERTS, dtype=jnp.int32), gate_weight, up_weight, down_weight))
    back = jnp.transpose(outs, (1, 0, 2, 3)).reshape(LINES, EXPERTS * CAPS, D)

    def one_line(items):
        table, values, gains, rows = items
        picked = jnp.einsum("skm,md->skd", table, values, precision=lax.Precision.HIGHEST)
        moe = jnp.sum(gains[:, :, None] * picked, axis=1)
        return (rows.astype(jnp.float32) + moe).astype(jnp.bfloat16)

    return lax.map(one_line, (gathers, back, route_gain, hidden_rows))
```

```python
import functools

import jax
import jax.numpy as jnp
from jax import lax
from jax.experimental import pallas as pl
from jax.experimental.pallas import tpu as pltpu
from jax.sharding import PartitionSpec as P

MESH = pl.DeviceIdType.MESH
NT = (((1,), (1,)), ((), ()))
F32, BF16 = jnp.float32, jnp.bfloat16

REL = (0, 1, -1, 2, -2, 3, -3, 4)
AT = {r: i for i, r in enumerate(REL)}
SPAN = ((0, 1), (1, 2), (3, 2), (5, 2), (7, 1))
ZS, YS, GS, CAPS, SLAB = 8, 4, 4, 16, 64


def kernel(
    meta_ref, hid, wg, wu, wd, out,
    meta, rows, x_all, y_out, w_gu, w_d, sel, mix, gu, gu_out, gu_in, act,
    own, other, x_in, q_out, back, z_out, z_in, fin, fin_own, fin_in, result,
    sa, ra, sm, rm, sz, rz, sy, ry, sx, rx, sp, rp, sxb, rxb, syb, ryb, szb, rzb, sf, rf, sl,
):
    g, a, e = lax.axis_index("grp"), lax.axis_index("attn"), lax.axis_index("exp")
    z, y = e // YS, e % YS
    h = g % 2
    half = own.shape[-1]
    part = half // 2

    def at_x(d):
        return ((g + d + GS) % GS, a, e)

    def at_y(d):
        return (g, a, z * YS + (y + d + YS) % YS)

    def at_z(d):
        return (g, a, ((z + d + ZS) % ZS) * YS + y)

    core = (g, 1 - a, e)

    def cols(c, base=0):
        return pl.ds(base + c * part, part)

    started = []

    def send(src, dst, ss, rs, dev):
        copy = pltpu.make_async_remote_copy(
            src_ref=src, dst_ref=dst, send_sem=ss, recv_sem=rs, device_id=dev, device_id_type=MESH
        )
        copy.start()
        started.append(copy)
        return copy

    peers = [at_x(d) for d in (1, 2, 3)] + [at_y(d) for d in (1, 2, 3)]
    peers += [at_z(r) for r in REL[1:]] + [core]
    barrier = pltpu.get_barrier_semaphore()
    for dev in peers:
        pl.semaphore_signal(barrier, inc=1, device_id=dev, device_id_type=MESH)

    mine, theirs = h * half, (1 - h) * half
    local = []

    def load(src, dst):
        copy = pltpu.make_async_copy(src, dst, sl.at[len(local)])
        copy.start()
        local.append(copy)
        return copy

    my_rows = pl.ds(pl.multiple_of(g * 16, 16), 16)
    firsts = [
        load(hid.at[:, pl.ds(pl.multiple_of(mine + c * part, 128), part)], rows.at[c, 0, my_rows, :])
        for c in (0, 1)
    ]
    pl.semaphore_wait(barrier, len(peers))

    xa = {}
    for c in (0, 1):
        for d in (1, 3, 2):
            there = ((g + d) % 2) * half + c * part
            xa[c, d] = send(
                hid.at[:, pl.ds(pl.multiple_of(there, 128), part)],
                rows.at[c, 0, my_rows, :], sa.at[c, d - 1], ra.at[c, d - 1], at_x(d),
            )
    xm = {}
    for r in REL[1:]:
        back_at = AT[-r] if r != 4 else AT[4]
        xm[r] = send(meta_ref, meta.at[back_at], sm.at[AT[r] - 1], rm.at[AT[r] - 1], at_z(r))
    weights = []
    for src, dst in ((wg, w_gu.at[pl.ds(0, wg.shape[0])]), (wu, w_gu.at[pl.ds(wg.shape[0], wg.shape[0])]), (wd, w_d)):
        for at, start in ((0, mine), (half, theirs)):
            weights.append(load(src.at[:, pl.ds(pl.multiple_of(start, 128), half)], dst.at[:, pl.ds(at, half)]))
    meta[0] = meta_ref[...]

    slots = YS * CAPS
    slot = lax.broadcasted_iota(jnp.int32, (slots, 128), 0)
    expert = (z * YS + (y + slot // CAPS) % YS).astype(F32)
    place = (lax.broadcasted_iota(jnp.int32, (slots, SLAB), 0) % CAPS).astype(F32)
    r_in = lax.broadcasted_iota(jnp.int32, (SLAB, SLAB), 0)
    r_out = lax.broadcasted_iota(jnp.int32, (SLAB, SLAB), 1)
    earlier = (r_in < r_out).astype(F32).astype(BF16)
    eye = (r_in == r_out).astype(F32).astype(BF16)

    def table(i):
        block = meta[i]
        picks = jnp.zeros((slots, 128), F32)
        gains = jnp.zeros((slots, 128), F32)
        for k in range(6):
            hit = block[k : k + 1, :] == expert
            picks = jnp.where(hit, 1.0, picks)
            gains = gains + jnp.where(hit, block[8 + k : 9 + k, :], 0.0)
        picks, gains = picks[:, :SLAB], gains[:, :SLAB]
        before = jnp.dot(picks.astype(BF16), earlier, preferred_element_type=F32)
        here = jnp.where(before == place, picks, 0.0)
        sel[i] = here.astype(BF16)
        weighed = (here * gains).astype(BF16)
        mix[i] = lax.dot_general(eye, weighed, NT, preferred_element_type=F32).astype(BF16)

    zd, yd, xd, pd, xb, yb, zb, fb = {}, {}, {}, {}, {}, {}, {}, {}

    def z_send(s, c):
        for sign, k in ((1, 0), (-1, 1)):
            if s == 4 and c != k:
                continue
            src = AT[-sign * (s - 1)]
            dst = AT[-sign * s] if s < 4 else AT[4]
            zd[s, c, k] = send(rows.at[c, src], rows.at[c, dst], sz.at[c, k, s - 1], rz.at[c, k, s - 1], at_z(sign))

    def z_event(s, c):
        if s == 0:
            firsts[c].wait()
            for d in (1, 2, 3):
                xa[c, d].wait_recv()
        else:
            for k in (0, 1):
                if (s, c, k) in zd:
                    zd[s, c, k].wait_recv()
        if s < 4:
            z_send(s + 1, c)

    def select(s, c):
        i0, n = SPAN[s]
        for i in range(i0, i0 + n):
            got = jnp.dot(sel[i], rows[c, i], preferred_element_type=F32).astype(BF16)
            x_all[i, 0, :, cols(c)] = got[0:CAPS]
            for d in (1, 2, 3):
                y_out[i, d - 1, :, cols(c)] = got[d * CAPS : (d + 1) * CAPS]
        for d in (1, 3, 2):
            yd[s, c, d] = send(
                y_out.at[pl.ds(i0, n), d - 1, :, cols(c)], x_all.at[pl.ds(i0, n), YS - d, :, cols(c)],
                sy.at[c, s, d - 1], ry.at[c, s, d - 1], at_y(d),
            )

    def y_event(s, c):
        for d in (1, 3, 2):
            yd[s, c, d].wait_recv()
        i0, n = SPAN[s]
        for k, step in ((0, 1), (1, -1)):
            lines, blocks = (pl.ds(i0 + k, 1), pl.ds(0, YS)) if n == 2 else (pl.ds(i0, 1), pl.ds(2 * k, 2))
            xd[s, c, k] = send(
                x_all.at[lines, blocks, :, cols(c)], x_all.at[lines, blocks, :, cols(c, half)],
                sx.at[c, s, k], rx.at[c, s, k], at_x(step),
            )

    def x_event(s):
        for c in (0, 1):
            for k in (0, 1):
                xd[s, c, k].wait_recv()

    def project(i0, n, number):
        at = pl.ds(i0 * SLAB, n * SLAB)
        block = x_all[pl.ds(i0, n)].reshape(n * SLAB, 2 * half)
        made = lax.dot_general(block, w_gu[...], NT, preferred_element_type=F32)
        gu[at] = made
        gu_out[at] = made.astype(BF16)
        pd[number] = send(gu_out.at[at], gu_in.at[at], sp.at[number], rp.at[number], core)

    def activate(i0, n, number):
        pd[number].wait_recv()
        at = pl.ds(i0 * SLAB, n * SLAB)
        total = gu[at] + gu_in[at].astype(F32)
        ff = total.shape[1] // 2
        gate, up = total[:, :ff], total[:, ff:]
        act[at] = (gate / (1.0 + jnp.exp(-gate)) * up).astype(BF16)

    def down(s):
        i0, n = SPAN[s]
        block = act[pl.ds(i0 * SLAB, n * SLAB)]
        for c in (0, 1):
            made = jnp.dot(block, w_d[:, cols(c, half)], preferred_element_type=F32).astype(BF16)
            other[pl.ds(i0, n), :, :, cols(c)] = made.reshape(n, YS, CAPS, part)
            for k, step in ((0, 1), (1, -1)):
                lines, blocks = (pl.ds(i0 + k, 1), pl.ds(0, YS)) if n == 2 else (pl.ds(i0, 1), pl.ds(2 * k, 2))
                xb[s, c, k] = send(
                    other.at[lines, blocks, :, cols(c)], x_in.at[lines, blocks, :, cols(c)],
                    sxb.at[c, s, k], rxb.at[c, s, k], at_x(step),
                )
        for c in (0, 1):
            made = jnp.dot(block, w_d[:, cols(c)], preferred_element_type=F32)
            own[pl.ds(i0, n), :, :, cols(c)] = made.reshape(n, YS, CAPS, part)

    def xb_event(s, c):
        for k in (0, 1):
            xb[s, c, k].wait_recv()
        i0, n = SPAN[s]
        at = pl.ds(i0, n)
        total = (own[at, :, :, cols(c)] + x_in[at, :, :, cols(c)].astype(F32)).astype(BF16)
        back[at, 0, :, cols(c)] = total[:, 0]
        for d in (1, 2, 3):
            q_out[at, d - 1, :, cols(c)] = total[:, d]
        for d in (1, 3, 2):
            yb[s, c, d] = send(
                q_out.at[at, d - 1, :, cols(c)], back.at[at, YS - d, :, cols(c)],
                syb.at[c, s, d - 1], ryb.at[c, s, d - 1], at_y(d),
            )

    def yb_event(s, c):
        for d in (1, 3, 2):
            yb[s, c, d].wait_recv()
        i0, n = SPAN[s]
        if s == 0:
            total = jnp.dot(mix[0], back[0, :, :, cols(c)].reshape(slots, part), preferred_element_type=F32)
            for k in (0, 1):
                zb[1, c, k].wait_recv()
                total = total + z_in[c, k, 0].astype(F32)
            fin[c] = total.astype(BF16)
            for d in (1, 3, 2):
                to_rows = pl.ds(pl.multiple_of(((g + d) % GS) * 16, 16), 16)
                fb[c, d] = send(fin.at[c, to_rows], fin_in.at[c, d - 1], sf.at[c, d - 1], rf.at[c, d - 1], at_x(d))
            return
        for sign, k in ((1, 0), (-1, 1)):
            if s == 4 and c != k:
                continue
            i = AT[sign * s] if s < 4 else AT[4]
            total = jnp.dot(mix[i], back[i, :, :, cols(c)].reshape(slots, part), preferred_element_type=F32)
            if (s + 1, c, k) in zb:
                zb[s + 1, c, k].wait_recv()
                total = total + z_in[c, k, s].astype(F32)
            z_out[c, k, s - 1] = total.astype(BF16)
            zb[s, c, k] = send(
                z_out.at[c, k, s - 1], z_in.at[c, k, s - 1], szb.at[c, k, s - 1], rzb.at[c, k, s - 1], at_z(sign)
            )

    table(0)
    for c in (0, 1):
        z_event(0, c)
        select(0, c)
    for r in REL[1:]:
        xm[r].wait_recv()
    for i in range(1, ZS):
        table(i)
    z_event(1, 0)
    select(1, 0)
    y_event(0, 0)
    z_event(1, 1)
    select(1, 1)
    y_event(0, 1)
    z_event(2, 0)
    select(2, 0)
    y_event(1, 0)
    z_event(2, 1)
    select(2, 1)
    y_event(1, 1)
    for copy in weights:
        copy.wait()
    z_event(3, 0)
    select(3, 0)
    y_event(2, 0)
    z_event(3, 1)
    select(3, 1)
    y_event(2, 1)
    x_event(0)
    x_event(1)
    project(0, 3, 0)
    z_event(4, 0)
    select(4, 0)
    y_event(3, 0)
    z_event(4, 1)
    select(4, 1)
    y_event(3, 1)
    x_event(2)
    project(3, 2, 1)
    y_event(4, 0)
    y_event(4, 1)
    x_event(3)
    project(5, 2, 2)
    x_event(4)
    project(7, 1, 3)
    activate(5, 2, 2)
    down(3)
    activate(7, 1, 3)
    down(4)
    xb_event(3, 0)
    xb_event(3, 1)
    activate(3, 2, 1)
    down(2)
    xb_event(4, 0)
    xb_event(4, 1)
    activate(0, 3, 0)
    down(1)
    yb_event(4, 0)
    yb_event(4, 1)
    xb_event(2, 0)
    xb_event(2, 1)
    yb_event(3, 0)
    yb_event(3, 1)
    down(0)
    xb_event(1, 0)
    xb_event(1, 1)
    yb_event(2, 0)
    yb_event(2, 1)
    xb_event(0, 0)
    xb_event(0, 1)
    yb_event(1, 0)
    yb_event(1, 1)
    yb_event(0, 0)
    yb_event(0, 1)

    for c in (0, 1):
        for d in (1, 2, 3):
            fb[c, d].wait_recv()
        result[:, cols(c)] = fin[c, my_rows].astype(F32) + fin_in[c, 1].astype(F32)
        result[:, cols(c, half)] = fin_in[c, 0].astype(F32) + fin_in[c, 2].astype(F32)
    stores = []
    for at, start in ((0, mine), (half, theirs)):
        stores.append(load(result.at[:, pl.ds(at, half)], out.at[:, pl.ds(pl.multiple_of(start, 128), half)]))
    for copy in started:
        copy.wait_send()
    for copy in stores:
        copy.wait()


def body(hidden_rows, routes, route_gain, gate_weight, up_weight, down_weight):
    hid = hidden_rows[0]
    n, width = hid.shape
    ff = gate_weight.shape[1]
    half = width // 2
    part = half // 2
    picked = routes[0].astype(F32).T
    gains = route_gain[0].T
    pad = ((0, 2), (0, 128 - SLAB))
    meta = jnp.concatenate([jnp.pad(picked, pad, constant_values=-1.0), jnp.pad(gains, pad)], axis=0)
    total = ZS * SLAB
    vmem = pltpu.VMEM
    dma = pltpu.SemaphoreType.DMA
    pair = lambda *shape: [dma(shape), dma(shape)]
    any_spec = pl.BlockSpec(memory_space=pl.ANY)
    moe = pl.pallas_call(
        kernel,
        out_shape=jax.ShapeDtypeStruct((n, width), F32),
        in_specs=[pl.BlockSpec(memory_space=pltpu.VMEM)] + [any_spec] * 4,
        out_specs=any_spec,
        scratch_shapes=[
            vmem((ZS, 16, 128), F32),
            vmem((2, ZS, SLAB, part), BF16),
            vmem((ZS, YS, CAPS, width), BF16),
            vmem((ZS, 3, CAPS, half), BF16),
            vmem((2 * ff, width), BF16),
            vmem((ff, width), BF16),
            vmem((ZS, YS * CAPS, SLAB), BF16),
            vmem((ZS, SLAB, YS * CAPS), BF16),
            vmem((total, 2 * ff), F32),
            vmem((total, 2 * ff), BF16),
            vmem((total, 2 * ff), BF16),
            vmem((total, ff), BF16),
            vmem((ZS, YS, CAPS, half), F32),
            vmem((ZS, YS, CAPS, half), BF16),
            vmem((ZS, YS, CAPS, half), BF16),
            vmem((ZS, 3, CAPS, half), BF16),
            vmem((ZS, YS, CAPS, half), BF16),
            vmem((2, 2, 4, SLAB, part), BF16),
            vmem((2, 2, 4, SLAB, part), BF16),
            vmem((2, SLAB, part), BF16),
            vmem((2, 16, part), BF16),
            vmem((2, 3, 16, part), BF16),
            vmem((n, width), F32),
            *pair(2, 3), *pair(7), *pair(2, 2, 4), *pair(2, 5, 3), *pair(2, 5, 2), *pair(4),
            *pair(2, 5, 2), *pair(2, 5, 3), *pair(2, 2, 4), *pair(2, 3), dma((10,)),
        ],
        compiler_params=pltpu.CompilerParams(
            collective_id=0, has_side_effects=True, vmem_limit_bytes=60 * 1024 * 1024
        ),
        name="routed_layer",
    )(meta, hid, gate_weight[0], up_weight[0], down_weight[0])
    return (hid.astype(F32) + moe).astype(BF16)[None]


def solution(mesh):
    placed = (
        P("exp", "grp", "attn"),
        P("exp", None, None),
        P("exp", None, None),
        P("exp", "grp", "attn"),
        P("exp", "grp", "attn"),
        P("exp", "grp", "attn"),
    )
    return jax.shard_map(
        body, mesh=mesh, in_specs=placed, out_specs=P("exp", "grp", "attn"), check_vma=False
    )
```

```python
import functools

import jax
import jax.numpy as jnp
from jax import lax
from jax.experimental import pallas as pl
from jax.experimental.pallas import tpu as pltpu
from jax.sharding import PartitionSpec as P

MESH = pl.DeviceIdType.MESH
NT = (((1,), (1,)), ((), ()))
F32, BF16 = jnp.float32, jnp.bfloat16

REL = (0, 1, -1, 2, -2, 3, -3, 4)
AT = {r: i for i, r in enumerate(REL)}
SPAN = ((0, 1), (1, 2), (3, 2), (5, 2), (7, 1))
ZS, YS, GS, CAPS, SLAB = 8, 4, 4, 16, 64
PIECES = ((0, 5), (5, 5))
FAR = (0, 1)
CS = range(len(PIECES))
WAYS = ((1, 0), (-1, 1))

ORDER = (
    ("table", 0), ("z_event", 0, 0), ("select", 0, 0), ("z_event", 0, 1), ("select", 0, 1), ("tables",),
    ("z_event", 1, 0), ("select", 1, 0), ("y_event", 0, 0), ("y_event", 0, 1), ("z_event", 1, 1), ("select", 1, 1),
    ("z_event", 2, 0), ("select", 2, 0), ("y_event", 1, 0), ("z_event", 2, 1), ("select", 2, 1), ("y_event", 1, 1),
    ("z_event", 3, 0), ("select", 3, 0), ("y_event", 2, 0), ("z_event", 3, 1), ("select", 3, 1), ("y_event", 2, 1),
    ("loaded",), ("x_event", 0), ("x_event", 1), ("project", 0, 3, 0), ("z_event", 4, 0), ("select", 4, 0),
    ("z_event", 4, 1), ("select", 4, 1), ("y_event", 3, 0), ("y_event", 3, 1), ("x_event", 2),
    ("project", 3, 2, 1), ("y_event", 4, 0), ("y_event", 4, 1), ("activate", 0, 3, 0), ("x_event", 3),
    ("project", 5, 2, 2), ("x_event", 4), ("project", 7, 1, 3), ("activate", 5, 2, 2), ("activate", 7, 1, 3),
    ("down", 4), ("down", 3), ("activate", 3, 2, 1), ("down", 2), ("xb_event", 4, 0), ("xb_event", 4, 1),
    ("xb_event", 3, 0), ("xb_event", 3, 1), ("down", 1), ("yb_event", 4, 0), ("yb_event", 4, 1),
    ("xb_event", 2, 0), ("xb_event", 2, 1), ("down", 0), ("yb_event", 3, 0), ("yb_event", 3, 1),
    ("xb_event", 1, 0), ("xb_event", 1, 1), ("yb_event", 2, 0), ("yb_event", 2, 1), ("xb_event", 0, 0),
    ("xb_event", 0, 1), ("yb_event", 0, 0), ("yb_event", 0, 1), ("yb_event", 1, 0), ("yb_event", 1, 1),
    ("finish", 0), ("finish", 1),
)


def kernel(
    routes_ref, gains_ref, hid, wg, wu, wd, out,
    meta, rows, x_all, y_out, w_gu, w_d, sel, mix, gu, gu_out, gu_in, act,
    own, other, x_in, q_out, back, z_out, z_in, fin, fin_in, residual, result,
    sent, ra, rm, rz, ry, rx, rp, rxb, ryb, rzb, rf, sl,
):
    g, a, e = lax.axis_index("grp"), lax.axis_index("attn"), lax.axis_index("exp")
    z, y = e // YS, e % YS
    h = g % 2
    half = own.shape[-1]

    def at_x(d):
        return ((g + d + GS) % GS, a, e)

    def at_zx(sign, d):
        return ((g + d) % GS, a, ((z + sign + ZS) % ZS) * YS + y)

    def at_y(d):
        return (g, a, z * YS + (y + d + YS) % YS)

    def at_z(d):
        return (g, a, ((z + d + ZS) % ZS) * YS + y)

    core = (g, 1 - a, e)

    def cols(c, base=0):
        first, size = PIECES[c]
        return pl.ds(base + first * 128, size * 128)

    def send(src, dst, ss, rs, dev):
        pltpu.make_async_remote_copy(
            src_ref=src, dst_ref=dst, send_sem=sent.at[ss], recv_sem=rs, device_id=dev, device_id_type=MESH
        ).start()

    def await_all(ref, sem):
        pltpu.make_async_copy(ref, ref, sem).wait()

    peers = [at_x(d) for d in (1, 2, 3)] + [at_y(d) for d in (1, 2, 3)]
    peers += [at_z(r) for r in REL[1:]] + [core]
    peers += [at_zx(sign, d) for sign in (1, -1) for d in (1, 2, 3)]
    barrier = pltpu.get_barrier_semaphore()
    for dev in peers:
        pl.semaphore_signal(barrier, inc=1, device_id=dev, device_id_type=MESH)

    mine, theirs = h * half, (1 - h) * half
    def load(src, dst, sem):
        pltpu.make_async_copy(src, dst, sem).start()

    meta[0] = jnp.full(meta.shape[1:], -1.0, F32)
    for k in range(6):
        meta[0, k : k + 1, :SLAB] = routes_ref[k].astype(F32)
        meta[0, 8 + k : 9 + k, :SLAB] = gains_ref[k]

    my_rows = pl.ds(pl.multiple_of(g * 16, 16), 16)
    load(hid.at[:, pl.ds(pl.multiple_of(mine, 128), half)], rows.at[0, my_rows, :], sl.at[0])
    pl.semaphore_wait(barrier, len(peers))

    for c in CS:
        for sign, first in ((1, 3), (-1, 7), (0, -1)):
            for d in (1, 3, 2, 0) if sign else (1, 3, 2):
                there = ((g + d) % 2) * half + PIECES[c][0] * 128
                n = first + d
                send(
                    hid.at[:, pl.ds(pl.multiple_of(there, 128), PIECES[c][1] * 128)],
                    rows.at[AT[-sign], my_rows, cols(c)], 0, ra.at[c, abs(sign)], at_zx(sign, d),
                )
    for r in REL[1:]:
        back_at = AT[-r] if r != 4 else AT[4]
        send(meta.at[0], meta.at[back_at], 1, rm.at[0], at_z(r))
    for at, start in ((0, mine), (half, theirs)):
        there, here = pl.ds(pl.multiple_of(start, 128), half), pl.ds(at, half)
        load(wg.at[:, there], w_gu.at[pl.ds(0, wg.shape[0]), here], sl.at[1])
        load(wu.at[:, there], w_gu.at[pl.ds(wg.shape[0], wg.shape[0]), here], sl.at[1])
        load(wd.at[:, there], w_d.at[:, here], sl.at[2])
        load(hid.at[:, there], residual.at[:, here], sl.at[3])

    slots = YS * CAPS
    slot = lax.broadcasted_iota(jnp.int32, (slots, 128), 0)
    expert = (z * YS + (y + slot // CAPS) % YS).astype(F32)
    place = (lax.broadcasted_iota(jnp.int32, (slots, SLAB), 0) % CAPS).astype(F32)
    r_in = lax.broadcasted_iota(jnp.int32, (SLAB, SLAB), 0)
    r_out = lax.broadcasted_iota(jnp.int32, (SLAB, SLAB), 1)
    earlier = (r_in < r_out).astype(F32).astype(BF16)
    eye = (r_in == r_out).astype(F32).astype(BF16)

    def table(i):
        block = meta[i]
        picks = jnp.zeros((slots, 128), F32)
        gains = jnp.zeros((slots, 128), F32)
        for k in range(6):
            hit = block[k : k + 1, :] == expert
            picks = jnp.where(hit, 1.0, picks)
            gains = gains + jnp.where(hit, block[8 + k : 9 + k, :], 0.0)
        picks, gains = picks[:, :SLAB], gains[:, :SLAB]
        before = jnp.dot(picks.astype(BF16), earlier, preferred_element_type=F32)
        here = jnp.where(before == place, picks, 0.0)
        sel[i] = here.astype(BF16)
        weighed = (here * gains).astype(BF16)
        mix[i] = lax.dot_general(eye, weighed, NT, preferred_element_type=F32).astype(BF16)

    def z_send(s, c):
        for sign, k in WAYS:
            if s == 4 and FAR[c] != k:
                continue
            src = AT[-sign * (s - 1)]
            dst = AT[-sign * s] if s < 4 else AT[4]
            send(rows.at[src, :, cols(c)], rows.at[dst, :, cols(c)], 2, rz.at[c, s - 2], at_z(sign))

    def z_event(s, c):
        i0, n = SPAN[s]
        if s == 0:
            if c == 0:
                await_all(rows.at[0, my_rows, :], sl.at[0])
            await_all(rows.at[0, pl.ds(0, SLAB - 16), cols(c)], ra.at[c, 0])
        else:
            await_all(rows.at[pl.ds(i0, n), :, cols(c)], ra.at[c, 1] if s == 1 else rz.at[c, s - 2])
        if 1 <= s < 4:
            z_send(s + 1, c)

    def select(s, c):
        i0, n = SPAN[s]
        for i in range(i0, i0 + n):
            got = jnp.dot(sel[i], rows[i, :, cols(c)], preferred_element_type=F32).astype(BF16)
            x_all[i, 0, :, cols(c)] = got[0:CAPS]
            for d in (1, 2, 3):
                y_out[i, d - 1, :, cols(c)] = got[d * CAPS : (d + 1) * CAPS]
        for d in (1, 3, 2):
            send(
                y_out.at[pl.ds(i0, n), d - 1, :, cols(c)], x_all.at[pl.ds(i0, n), YS - d, :, cols(c)],
                3, ry.at[c, s], at_y(d),
            )

    def y_event(s, c):
        i0, n = SPAN[s]
        await_all(x_all.at[pl.ds(i0, n), pl.ds(1, 3), :, cols(c)], ry.at[c, s])
        for k, step in ((0, 1), (1, -1)):
            lines, blocks = (pl.ds(i0 + k, 1), pl.ds(0, YS)) if n == 2 else (pl.ds(i0, 1), pl.ds(2 * k, 2))
            send(
                x_all.at[lines, blocks, :, cols(c)], x_all.at[lines, blocks, :, cols(c, half)],
                4, rx.at[s], at_x(step),
            )

    def x_event(s):
        i0, n = SPAN[s]
        await_all(x_all.at[pl.ds(i0, n), :, :, pl.ds(half, half)], rx.at[s])

    def project(i0, n, number):
        at = pl.ds(i0 * SLAB, n * SLAB)
        block = x_all[pl.ds(i0, n)].reshape(n * SLAB, 2 * half)
        made = lax.dot_general(block, w_gu[...], NT, preferred_element_type=F32)
        gu[at] = made
        gu_out[at] = made.astype(BF16)
        send(gu_out.at[at], gu_in.at[at], 5, rp.at[number], core)

    def activate(i0, n, number):
        at = pl.ds(i0 * SLAB, n * SLAB)
        await_all(gu_in.at[at], rp.at[number])
        total = gu[at] + gu_in[at].astype(F32)
        ff = total.shape[1] // 2
        gate, up = total[:, :ff], total[:, ff:]
        act[at] = (gate / (1.0 + jnp.exp(-gate)) * up).astype(BF16)

    def down(s):
        i0, n = SPAN[s]
        block = act[pl.ds(i0 * SLAB, n * SLAB)]
        for c in CS:
            made = jnp.dot(block, w_d[:, cols(c, half)], preferred_element_type=F32).astype(BF16)
            other[pl.ds(i0, n), :, :, cols(c)] = made.reshape(n, YS, CAPS, made.shape[-1])
            for k, step in ((0, 1), (1, -1)):
                lines, blocks = (pl.ds(i0 + k, 1), pl.ds(0, YS)) if n == 2 else (pl.ds(i0, 1), pl.ds(2 * k, 2))
                send(
                    other.at[lines, blocks, :, cols(c)], x_in.at[lines, blocks, :, cols(c)],
                    6, rxb.at[c, s], at_x(step),
                )
        for c in CS:
            made = jnp.dot(block, w_d[:, cols(c)], preferred_element_type=F32)
            own[pl.ds(i0, n), :, :, cols(c)] = made.reshape(n, YS, CAPS, made.shape[-1])

    def xb_event(s, c):
        i0, n = SPAN[s]
        at = pl.ds(i0, n)
        await_all(x_in.at[at, :, :, cols(c)], rxb.at[c, s])
        total = (own[at, :, :, cols(c)] + x_in[at, :, :, cols(c)].astype(F32)).astype(BF16)
        back[at, 0, :, cols(c)] = total[:, 0]
        for d in (1, 2, 3):
            q_out[at, d - 1, :, cols(c)] = total[:, d]
        for d in (1, 3, 2):
            send(
                q_out.at[at, d - 1, :, cols(c)], back.at[at, YS - d, :, cols(c)],
                7, ryb.at[c, s], at_y(d),
            )

    def yb_event(s, c):
        i0, n = SPAN[s]
        await_all(back.at[pl.ds(i0, n), pl.ds(1, 3), :, cols(c)], ryb.at[c, s])
        width = PIECES[c][1] * 128
        if s == 0:
            total = jnp.dot(mix[0], back[0, :, :, cols(c)].reshape(slots, width), preferred_element_type=F32)
            fin[:, cols(c)] = total.astype(BF16)
            spread(fin, c, 0, -1, (1, 3, 2))
            return
        first_way = FAR[c] if s == 3 else 0
        for sign, k in WAYS:
            if s == 4 and FAR[c] != k:
                continue
            i = AT[sign * s] if s < 4 else AT[4]
            total = jnp.dot(mix[i], back[i, :, :, cols(c)].reshape(slots, width), preferred_element_type=F32)
            if s < 3 or (s == 3 and FAR[c] == k):
                if k == first_way:
                    ways = pl.ds(0, 2) if s < 3 else pl.ds(k, 1)
                    await_all(z_in.at[ways, s - 1, :, cols(c)], rzb.at[c, s - 1])
                total = total + z_in[k, s - 1, :, cols(c)].astype(F32)
            z_out[k, s - 1, :, cols(c)] = total.astype(BF16)
            if s == 1:
                spread(z_out.at[k, 0], c, sign, 3 + 4 * k, (1, 3, 2, 0))
            else:
                send(
                    z_out.at[k, s - 1, :, cols(c)], z_in.at[k, s - 2, :, cols(c)],
                    8, rzb.at[c, s - 2], at_z(sign),
                )

    def spread(src, c, sign, first, far):
        for d in far:
            to_rows = pl.ds(pl.multiple_of(((g + d) % GS) * 16, 16), 16)
            n = first + d
            send(src.at[to_rows, cols(c)], fin_in.at[n, :, cols(c)], 9, rf.at[c], at_zx(sign, d))

    def tables():
        await_all(meta.at[pl.ds(1, ZS - 1)], rm.at[0])
        for i in range(1, ZS):
            table(i)

    def loaded():
        for ref, n in ((w_gu, 1), (w_d, 2), (residual, 3)):
            await_all(ref, sl.at[n])

    def finish(c):
        await_all(fin_in.at[:, :, cols(c)], rf.at[c])
        here, there = cols(c), cols(c, half)
        moe = fin[my_rows, here].astype(F32)
        for n in (1, 3, 5, 7, 9):
            moe = moe + fin_in[n, :, here].astype(F32)
        result[:, here] = (residual[:, here].astype(F32) + moe).astype(BF16)
        moe = fin_in[0, :, here].astype(F32)
        for n in (2, 4, 6, 8, 10):
            moe = moe + fin_in[n, :, here].astype(F32)
        result[:, there] = (residual[:, there].astype(F32) + moe).astype(BF16)

    steps = dict(
        table=table, tables=tables, z_event=z_event, select=select, y_event=y_event, loaded=loaded, x_event=x_event,
        project=project, activate=activate, down=down, xb_event=xb_event, yb_event=yb_event, finish=finish,
    )
    for step, *given in ORDER:
        steps[step](*given)
    for at, start in ((0, mine), (half, theirs)):
        load(result.at[:, pl.ds(at, half)], out.at[:, pl.ds(pl.multiple_of(start, 128), half)], sl.at[4])
    five = rows.at[pl.ds(0, 5)]
    sizes = (fin_in, meta.at[pl.ds(0, ZS - 1)], five, y_out, other, gu_out, other, q_out, five, fin_in)
    for n, ref in enumerate(sizes):
        await_all(ref, sent.at[n])
    await_all(result, sl.at[4])


def body(hidden_rows, routes, route_gain, gate_weight, up_weight, down_weight):
    hid = hidden_rows[0]
    n, width = hid.shape
    ff = gate_weight.shape[1]
    half = width // 2
    picked, gains = (jnp.transpose(v, (2, 0, 1)) for v in (routes, route_gain))
    total, n_c = ZS * SLAB, len(PIECES)
    vmem = pltpu.VMEM
    dma = pltpu.SemaphoreType.DMA
    any_spec = pl.BlockSpec(memory_space=pl.ANY)
    out = pl.pallas_call(
        kernel,
        out_shape=jax.ShapeDtypeStruct((n, width), BF16),
        in_specs=[pl.BlockSpec(memory_space=pltpu.VMEM)] * 2 + [any_spec] * 4,
        out_specs=any_spec,
        scratch_shapes=[
            vmem((ZS, 16, 128), F32),
            vmem((ZS, SLAB, half), BF16),
            vmem((ZS, YS, CAPS, width), BF16),
            vmem((ZS, 3, CAPS, half), BF16),
            vmem((2 * ff, width), BF16),
            vmem((ff, width), BF16),
            vmem((ZS, YS * CAPS, SLAB), BF16),
            vmem((ZS, SLAB, YS * CAPS), BF16),
            vmem((total, 2 * ff), F32),
            vmem((total, 2 * ff), BF16),
            vmem((total, 2 * ff), BF16),
            vmem((total, ff), BF16),
            vmem((ZS, YS, CAPS, half), F32),
            vmem((ZS, YS, CAPS, half), BF16),
            vmem((ZS, YS, CAPS, half), BF16),
            vmem((ZS, 3, CAPS, half), BF16),
            vmem((ZS, YS, CAPS, half), BF16),
            vmem((2, 4, SLAB, half), BF16),
            vmem((2, 3, SLAB, half), BF16),
            vmem((SLAB, half), BF16),
            vmem((11, 16, half), BF16),
            vmem((n, width), BF16),
            vmem((n, width), BF16),
            dma((10,)), dma((n_c, 2)), dma((1,)), dma((n_c, 3)), dma((n_c, 5)), dma((5,)), dma((4,)),
            dma((n_c, 5)), dma((n_c, 5)), dma((n_c, 3)), dma((n_c,)), dma((5,)),
        ],
        compiler_params=pltpu.CompilerParams(
            collective_id=0, has_side_effects=True, vmem_limit_bytes=60 * 1024 * 1024
        ),
        name="routed_layer",
    )(picked, gains, hid, gate_weight[0], up_weight[0], down_weight[0])
    return out[None]


def solution(mesh):
    placed = (
        P("exp", "grp", "attn"),
        P("exp", None, None),
        P("exp", None, None),
        P("exp", "grp", "attn"),
        P("exp", "grp", "attn"),
        P("exp", "grp", "attn"),
    )
    return jax.shard_map(
        body, mesh=mesh, in_specs=placed, out_specs=P("exp", "grp", "attn"), check_vma=False
    )
```

```python
import functools

import jax
import jax.numpy as jnp
from jax import lax
from jax.experimental import pallas as pl
from jax.experimental.pallas import tpu as pltpu
from jax.sharding import PartitionSpec as P

MESH = pl.DeviceIdType.MESH
NT = (((1,), (1,)), ((), ()))
F32, BF16 = jnp.float32, jnp.bfloat16

REL = (0, 1, -1, 2, -2, 3, -3, 4)
AT = {r: i for i, r in enumerate(REL)}
SPAN = ((0, 1), (1, 2), (3, 2), (5, 2), (7, 1))
ZS, YS, GS, CAPS, SLAB = 8, 4, 4, 16, 64
PIECES = ((0, 3), (3, 2), (5, 3), (8, 2))
FAR = (0, 1, 1, 0)
CS = range(len(PIECES))
PAIRS = ((0, 5), (5, 5))
WAYS = ((1, 0), (-1, 1))

ORDER = (
    ("table", 0), ("z_event", 0, 0), ("z_event", 0, 1), ("z_event", 0, 2), ("z_event", 0, 3), ("select", 0, 0),
    ("select", 0, 1), ("z_event", 1, 0), ("z_event", 1, 1), ("z_event", 1, 2), ("z_event", 1, 3), ("tables",),
    ("table", 1), ("table", 2), ("select", 1, 0), ("select", 1, 1), ("table", 3), ("table", 4), ("z_event", 2, 0),
    ("z_event", 2, 1), ("select", 2, 0), ("z_event", 2, 2), ("z_event", 2, 3), ("select", 2, 1), ("y_event", 0, 0),
    ("y_event", 0, 1), ("y_event", 1, 0), ("y_event", 1, 1), ("table", 5), ("table", 6), ("z_event", 3, 0),
    ("z_event", 3, 1), ("select", 3, 0), ("z_event", 3, 2), ("z_event", 3, 3), ("select", 3, 1), ("table", 7),
    ("y_event", 2, 0), ("y_event", 2, 1), ("loaded",), ("project_own", 0, 3), ("z_event", 4, 0), ("z_event", 4, 1),
    ("select", 4, 0), ("z_event", 4, 2), ("z_event", 4, 3), ("select", 4, 1), ("x_event", 0), ("x_event", 1),
    ("project", 0, 3, 0), ("y_event", 3, 0), ("y_event", 3, 1), ("project_own", 3, 2), ("y_event", 4, 0),
    ("y_event", 4, 1), ("x_event", 2), ("project", 3, 2, 1), ("project_own", 5, 2), ("project_own", 7, 1),
    ("activate", 0, 3, 0), ("down", 1), ("activate", 3, 2, 1), ("weigh", 7), ("weigh", 5), ("weigh", 6),
    ("weigh", 3), ("weigh", 4), ("weigh", 1), ("weigh", 2), ("weigh", 0), ("x_event", 3), ("project", 5, 2, 2),
    ("x_event", 4), ("project", 7, 1, 3), ("activate", 5, 2, 2), ("activate", 7, 1, 3), ("down", 4), ("down", 3),
    ("xb_event", 4, 0), ("xb_event", 4, 1), ("down", 2), ("xb_event", 3, 0), ("xb_event", 3, 1),
    ("yb_event", 4, 0), ("yb_event", 4, 1), ("yb_event", 4, 2), ("yb_event", 4, 3), ("xb_event", 1, 0),
    ("xb_event", 1, 1), ("down", 0), ("xb_event", 2, 0), ("xb_event", 2, 1), ("yb_event", 3, 0),
    ("yb_event", 3, 1), ("yb_event", 3, 2), ("yb_event", 3, 3), ("xb_event", 0, 0), ("xb_event", 0, 1),
    ("yb_event", 2, 0), ("yb_event", 2, 1), ("yb_event", 2, 2), ("yb_event", 2, 3), ("yb_event", 0, 0),
    ("yb_event", 0, 1), ("yb_event", 0, 2), ("yb_event", 0, 3), ("yb_event", 1, 0), ("yb_event", 1, 1),
    ("yb_event", 1, 2), ("yb_event", 1, 3), ("finish", 0), ("finish", 1), ("finish", 2), ("finish", 3),
)


def kernel(
    routes_ref, gains_ref, hid, wg, wu, wd, out,
    meta, rows, x_all, y_out, w_gu, w_d, sel, mix, gu, gu_out, gu_in, act,
    own, other, x_in, q_out, back, z_out, z_in, fin, fin_in, residual,
    sent, ra, rm, rz, ry, rx, rp, rxb, ryb, rzb, rf, sl,
):
    g, a, e = lax.axis_index("grp"), lax.axis_index("attn"), lax.axis_index("exp")
    z, y = e // YS, e % YS
    h = g % 2
    half = own.shape[-1]

    def at_x(d):
        return ((g + d + GS) % GS, a, e)

    def at_zx(sign, d):
        return ((g + d) % GS, a, ((z + sign + ZS) % ZS) * YS + y)

    def at_y(d):
        return (g, a, z * YS + (y + d + YS) % YS)

    def at_z(d):
        return (g, a, ((z + d + ZS) % ZS) * YS + y)

    core = (g, 1 - a, e)

    def cols(c, base=0):
        first, size = PIECES[c]
        return pl.ds(base + first * 128, size * 128)

    def pair(c, base=0):
        first, size = PAIRS[c]
        return pl.ds(base + first * 128, size * 128)

    def send(src, dst, ss, rs, dev):
        pltpu.make_async_remote_copy(
            src_ref=src, dst_ref=dst, send_sem=sent.at[ss], recv_sem=rs, device_id=dev, device_id_type=MESH
        ).start()

    def await_all(ref, sem):
        pltpu.make_async_copy(ref, ref, sem).wait()

    peers = [at_x(d) for d in (1, 2, 3)] + [at_y(d) for d in (1, 2, 3)]
    peers += [at_z(r) for r in REL[1:]] + [core]
    peers += [at_zx(sign, d) for sign in (1, -1) for d in (1, 2, 3)]
    barrier = pltpu.get_barrier_semaphore()
    for dev in peers:
        pl.semaphore_signal(barrier, inc=1, device_id=dev, device_id_type=MESH)

    mine, theirs = h * half, (1 - h) * half
    def load(src, dst, sem):
        pltpu.make_async_copy(src, dst, sem).start()

    meta[0] = jnp.full(meta.shape[1:], -1.0, F32)
    for k in range(6):
        meta[0, k : k + 1, :SLAB] = routes_ref[k].astype(F32)
        meta[0, 8 + k : 9 + k, :SLAB] = gains_ref[k]

    my_rows = pl.ds(pl.multiple_of(g * 16, 16), 16)
    load(hid.at[:, pl.ds(pl.multiple_of(mine, 128), half)], rows.at[0, my_rows, :], sl.at[0])
    pl.semaphore_wait(barrier, len(peers))

    for c in CS:
        for sign, first in ((1, 3), (-1, 7), (0, -1)):
            for d in (1, 3, 2, 0) if sign else (1, 3, 2):
                there = ((g + d) % 2) * half + PIECES[c][0] * 128
                n = first + d
                send(
                    hid.at[:, pl.ds(pl.multiple_of(there, 128), PIECES[c][1] * 128)],
                    rows.at[AT[-sign], my_rows, cols(c)], 0, ra.at[c, abs(sign)], at_zx(sign, d),
                )
    for r in REL[1:]:
        back_at = AT[-r] if r != 4 else AT[4]
        send(meta.at[0], meta.at[back_at], 1, rm.at[0], at_z(r))
    for at, start in ((0, mine), (half, theirs)):
        there, here = pl.ds(pl.multiple_of(start, 128), half), pl.ds(at, half)
        load(wg.at[:, there], w_gu.at[pl.ds(0, wg.shape[0]), here], sl.at[1])
        load(wu.at[:, there], w_gu.at[pl.ds(wg.shape[0], wg.shape[0]), here], sl.at[1])
        load(wd.at[:, there], w_d.at[:, here], sl.at[2])
        load(hid.at[:, there], residual.at[:, here], sl.at[3])

    slots = YS * CAPS
    slot = lax.broadcasted_iota(jnp.int32, (slots, 128), 0)
    expert = (z * YS + (y + slot // CAPS) % YS).astype(F32)
    place = (lax.broadcasted_iota(jnp.int32, (slots, SLAB), 0) % CAPS).astype(F32)
    r_in = lax.broadcasted_iota(jnp.int32, (SLAB, SLAB), 0)
    r_out = lax.broadcasted_iota(jnp.int32, (SLAB, SLAB), 1)
    earlier = (r_in < r_out).astype(F32).astype(BF16)
    eye = (r_in == r_out).astype(F32).astype(BF16)

    def table(i):
        block = meta[i]
        picks = jnp.zeros((slots, 128), F32)
        for k in range(6):
            picks = jnp.where(block[k : k + 1, :] == expert, 1.0, picks)
        picks = picks[:, :SLAB]
        before = jnp.dot(picks.astype(BF16), earlier, preferred_element_type=F32)
        sel[i] = jnp.where(before == place, picks, 0.0).astype(BF16)

    def weigh(i):
        block = meta[i]
        gains = jnp.zeros((slots, 128), F32)
        for k in range(6):
            gains = jnp.where(block[k : k + 1, :] == expert, block[8 + k : 9 + k, :], gains)
        weighed = (sel[i].astype(F32) * gains[:, :SLAB]).astype(BF16)
        mix[i] = lax.dot_general(eye, weighed, NT, preferred_element_type=F32).astype(BF16)

    def z_send(s, c):
        for sign, k in WAYS:
            if s == 4 and FAR[c] != k:
                continue
            src = AT[-sign * (s - 1)]
            dst = AT[-sign * s] if s < 4 else AT[4]
            send(rows.at[src, :, cols(c)], rows.at[dst, :, cols(c)], 2, rz.at[c, s - 2], at_z(sign))

    def z_event(s, c):
        i0, n = SPAN[s]
        if s == 0:
            if c == 0:
                await_all(rows.at[0, my_rows, :], sl.at[0])
            await_all(rows.at[0, pl.ds(0, SLAB - 16), cols(c)], ra.at[c, 0])
        else:
            await_all(rows.at[pl.ds(i0, n), :, cols(c)], ra.at[c, 1] if s == 1 else rz.at[c, s - 2])
        if 1 <= s < 4:
            z_send(s + 1, c)

    def select(s, c):
        i0, n = SPAN[s]
        for i in range(i0, i0 + n):
            got = jnp.dot(sel[i], rows[i, :, pair(c)], preferred_element_type=F32).astype(BF16)
            x_all[i, 0, :, pair(c)] = got[0:CAPS]
            for d in (1, 2, 3):
                y_out[i, d - 1, :, pair(c)] = got[d * CAPS : (d + 1) * CAPS]
        for d in (1, 3, 2):
            send(
                y_out.at[pl.ds(i0, n), d - 1, :, pair(c)], x_all.at[pl.ds(i0, n), YS - d, :, pair(c)],
                3, ry.at[c, s], at_y(d),
            )

    def y_event(s, c):
        i0, n = SPAN[s]
        await_all(x_all.at[pl.ds(i0, n), pl.ds(1, 3), :, pair(c)], ry.at[c, s])
        for k, step in ((0, 1), (1, -1)):
            lines, blocks = (pl.ds(i0 + k, 1), pl.ds(0, YS)) if n == 2 else (pl.ds(i0, 1), pl.ds(2 * k, 2))
            send(
                x_all.at[lines, blocks, :, pair(c)], x_all.at[lines, blocks, :, pair(c, half)],
                4, rx.at[s], at_x(step),
            )

    def x_event(s):
        i0, n = SPAN[s]
        await_all(x_all.at[pl.ds(i0, n), :, :, pl.ds(half, half)], rx.at[s])

    def project_own(i0, n):
        block = x_all[pl.ds(i0, n), :, :, pl.ds(0, half)].reshape(n * SLAB, half)
        gu[pl.ds(i0 * SLAB, n * SLAB)] = lax.dot_general(block, w_gu[:, :half], NT, preferred_element_type=F32)

    def project(i0, n, number):
        at = pl.ds(i0 * SLAB, n * SLAB)
        block = x_all[pl.ds(i0, n), :, :, pl.ds(half, half)].reshape(n * SLAB, half)
        made = gu[at] + lax.dot_general(block, w_gu[:, half:], NT, preferred_element_type=F32)
        gu[at] = made
        gu_out[at] = made.astype(BF16)
        send(gu_out.at[at], gu_in.at[at], 5, rp.at[number], core)

    def activate(i0, n, number):
        at = pl.ds(i0 * SLAB, n * SLAB)
        await_all(gu_in.at[at], rp.at[number])
        total = gu[at] + gu_in[at].astype(F32)
        ff = total.shape[1] // 2
        gate, up = total[:, :ff], total[:, ff:]
        act[at] = (gate / (1.0 + jnp.exp(-gate)) * up).astype(BF16)

    def down(s):
        i0, n = SPAN[s]
        block = act[pl.ds(i0 * SLAB, n * SLAB)]
        for c in (0, 1):
            made = jnp.dot(block, w_d[:, pair(c, half)], preferred_element_type=F32).astype(BF16)
            other[pl.ds(i0, n), :, :, pair(c)] = made.reshape(n, YS, CAPS, made.shape[-1])
            for k, step in ((0, 1), (1, -1)):
                lines, blocks = (pl.ds(i0 + k, 1), pl.ds(0, YS)) if n == 2 else (pl.ds(i0, 1), pl.ds(2 * k, 2))
                send(
                    other.at[lines, blocks, :, pair(c)], x_in.at[lines, blocks, :, pair(c)],
                    6, rxb.at[c, s], at_x(step),
                )
        for c in (0, 1):
            made = jnp.dot(block, w_d[:, pair(c)], preferred_element_type=F32)
            own[pl.ds(i0, n), :, :, pair(c)] = made.reshape(n, YS, CAPS, made.shape[-1])

    def xb_event(s, c):
        i0, n = SPAN[s]
        at = pl.ds(i0, n)
        await_all(x_in.at[at, :, :, pair(c)], rxb.at[c, s])
        total = (own[at, :, :, pair(c)] + x_in[at, :, :, pair(c)].astype(F32)).astype(BF16)
        back[at, 0, :, pair(c)] = total[:, 0]
        for d in (1, 2, 3):
            q_out[at, d - 1, :, pair(c)] = total[:, d]
        for d in (1, 3, 2):
            send(
                q_out.at[at, d - 1, :, pair(c)], back.at[at, YS - d, :, pair(c)],
                7, ryb.at[c, s], at_y(d),
            )

    def yb_event(s, c):
        i0, n = SPAN[s]
        if c % 2 == 0:
            await_all(back.at[pl.ds(i0, n), pl.ds(1, 3), :, pair(c // 2)], ryb.at[c // 2, s])
        width = PIECES[c][1] * 128
        if s == 0:
            total = jnp.dot(mix[0], back[0, :, :, cols(c)].reshape(slots, width), preferred_element_type=F32)
            fin[:, cols(c)] = total.astype(BF16)
            spread(fin, c, 0, -1, (1, 3, 2))
            return
        first_way = FAR[c] if s == 3 else 0
        for sign, k in WAYS:
            if s == 4 and FAR[c] != k:
                continue
            i = AT[sign * s] if s < 4 else AT[4]
            total = jnp.dot(mix[i], back[i, :, :, cols(c)].reshape(slots, width), preferred_element_type=F32)
            if s < 3 or (s == 3 and FAR[c] == k):
                if k == first_way:
                    ways = pl.ds(0, 2) if s < 3 else pl.ds(k, 1)
                    await_all(z_in.at[ways, s - 1, :, cols(c)], rzb.at[c, s - 1])
                total = total + z_in[k, s - 1, :, cols(c)].astype(F32)
            z_out[k, s - 1, :, cols(c)] = total.astype(BF16)
            if s == 1:
                spread(z_out.at[k, 0], c, sign, 3 + 4 * k, (1, 3, 2, 0))
            else:
                send(
                    z_out.at[k, s - 1, :, cols(c)], z_in.at[k, s - 2, :, cols(c)],
                    8, rzb.at[c, s - 2], at_z(sign),
                )

    def spread(src, c, sign, first, far):
        for d in far:
            to_rows = pl.ds(pl.multiple_of(((g + d) % GS) * 16, 16), 16)
            n = first + d
            send(src.at[to_rows, cols(c)], fin_in.at[n, :, cols(c)], 9, rf.at[c], at_zx(sign, d))

    def tables():
        await_all(meta.at[pl.ds(1, ZS - 1)], rm.at[0])

    def loaded():
        for ref, n in ((w_gu, 1), (w_d, 2), (residual, 3)):
            await_all(ref, sl.at[n])

    def finish(c):
        await_all(fin_in.at[:, :, cols(c)], rf.at[c])
        here, there = cols(c), cols(c, half)
        moe = fin[my_rows, here].astype(F32)
        for n in (1, 3, 5, 7, 9):
            moe = moe + fin_in[n, :, here].astype(F32)
        first, size = PIECES[c]
        at = pl.ds(pl.multiple_of(mine + first * 128, 128), size * 128)
        out[:, at] = (residual[:, here].astype(F32) + moe).astype(BF16)
        moe = fin_in[0, :, here].astype(F32)
        for n in (2, 4, 6, 8, 10):
            moe = moe + fin_in[n, :, here].astype(F32)
        at = pl.ds(pl.multiple_of(theirs + first * 128, 128), size * 128)
        out[:, at] = (residual[:, there].astype(F32) + moe).astype(BF16)

    steps = dict(
        table=table, tables=tables, weigh=weigh, z_event=z_event, select=select, y_event=y_event, loaded=loaded, x_event=x_event,
        project_own=project_own, project=project, activate=activate, down=down, xb_event=xb_event, yb_event=yb_event, finish=finish,
    )
    for step, *given in ORDER:
        steps[step](*given)
    five = rows.at[pl.ds(0, 5)]
    sizes = (fin_in, meta.at[pl.ds(0, ZS - 1)], five, y_out, other, gu_out, other, q_out, five, fin_in)
    for n, ref in enumerate(sizes):
        await_all(ref, sent.at[n])


def body(hidden_rows, routes, route_gain, gate_weight, up_weight, down_weight):
    hid = hidden_rows[0]
    n, width = hid.shape
    ff = gate_weight.shape[1]
    half = width // 2
    picked, gains = (jnp.transpose(v, (2, 0, 1)) for v in (routes, route_gain))
    total, n_c = ZS * SLAB, len(PIECES)
    vmem = pltpu.VMEM
    dma = pltpu.SemaphoreType.DMA
    any_spec = pl.BlockSpec(memory_space=pl.ANY)
    out = pl.pallas_call(
        kernel,
        out_shape=pltpu.VMEM((n, width), BF16),
        in_specs=[pl.BlockSpec(memory_space=pltpu.VMEM)] * 2 + [any_spec] * 4,
        out_specs=pl.BlockSpec(memory_space=pltpu.VMEM),
        scratch_shapes=[
            vmem((ZS, 16, 128), F32),
            vmem((ZS, SLAB, half), BF16),
            vmem((ZS, YS, CAPS, width), BF16),
            vmem((ZS, 3, CAPS, half), BF16),
            vmem((2 * ff, width), BF16),
            vmem((ff, width), BF16),
            vmem((ZS, YS * CAPS, SLAB), BF16),
            vmem((ZS, SLAB, YS * CAPS), BF16),
            vmem((total, 2 * ff), F32),
            vmem((total, 2 * ff), BF16),
            vmem((total, 2 * ff), BF16),
            vmem((total, ff), BF16),
            vmem((ZS, YS, CAPS, half), F32),
            vmem((ZS, YS, CAPS, half), BF16),
            vmem((ZS, YS, CAPS, half), BF16),
            vmem((ZS, 3, CAPS, half), BF16),
            vmem((ZS, YS, CAPS, half), BF16),
            vmem((2, 4, SLAB, half), BF16),
            vmem((2, 3, SLAB, half), BF16),
            vmem((SLAB, half), BF16),
            vmem((11, 16, half), BF16),
            vmem((n, width), BF16),
            dma((10,)), dma((n_c, 2)), dma((1,)), dma((n_c, 3)), dma((2, 5)), dma((5,)), dma((4,)),
            dma((2, 5)), dma((2, 5)), dma((n_c, 3)), dma((n_c,)), dma((4,)),
        ],
        compiler_params=pltpu.CompilerParams(
            collective_id=0, has_side_effects=True, vmem_limit_bytes=60 * 1024 * 1024
        ),
        name="routed_layer",
    )(picked, gains, hid, gate_weight[0], up_weight[0], down_weight[0])
    return out[None]


def solution(mesh):
    placed = (
        P("exp", "grp", "attn"),
        P("exp", None, None),
        P("exp", None, None),
        P("exp", "grp", "attn"),
        P("exp", "grp", "attn"),
        P("exp", "grp", "attn"),
    )
    return jax.shard_map(
        body, mesh=mesh, in_specs=placed, out_specs=P("exp", "grp", "attn"), check_vma=False
    )
```

```python
import functools

import jax
import jax.numpy as jnp
from jax import lax
from jax.experimental import pallas as pl
from jax.experimental.pallas import tpu as pltpu
from jax.sharding import PartitionSpec as P

MESH = pl.DeviceIdType.MESH
NT = (((1,), (1,)), ((), ()))
F32, BF16 = jnp.float32, jnp.bfloat16

REL = (0, 1, -1, 2, -2, 3, -3, 4)
AT = {r: i for i, r in enumerate(REL)}
SPAN = ((0, 1), (1, 2), (3, 2), (5, 2), (7, 1))
ZS, YS, GS, CAPS, SLAB = 8, 4, 4, 16, 64
PIECES = ((0, 3), (3, 2), (5, 3), (8, 2))
FAR = (0, 1, 1, 0)
CS = range(len(PIECES))
PAIRS = ((0, 5), (5, 5))
WAYS = ((1, 0), (-1, 1))

ORDER = (
    ("table", 0), ("z_event", 0, 0), ("z_event", 0, 1), ("z_event", 0, 2), ("z_event", 0, 3), ("tables",),
    ("table", 1), ("table", 2), ("z_event", 1, 0), ("z_event", 1, 1), ("z_event", 1, 2), ("z_event", 1, 3),
    ("select", 0, 0), ("select", 0, 1), ("select", 1, 0), ("select", 1, 1), ("table", 3), ("table", 4),
    ("z_event", 2, 0), ("z_event", 2, 1), ("select", 2, 0), ("z_event", 2, 2), ("z_event", 2, 3), ("select", 2, 1),
    ("y_event", 0, 0), ("y_event", 0, 1), ("y_event", 1, 0), ("y_event", 1, 1), ("table", 5), ("table", 6),
    ("z_event", 3, 0), ("z_event", 3, 1), ("select", 3, 0), ("z_event", 3, 2), ("z_event", 3, 3), ("select", 3, 1),
    ("table", 7), ("y_event", 2, 0), ("y_event", 2, 1), ("loaded",), ("project_own", 0, 3), ("z_event", 4, 0),
    ("z_event", 4, 1), ("select", 4, 0), ("z_event", 4, 2), ("z_event", 4, 3), ("select", 4, 1), ("x_event", 0),
    ("x_event", 1), ("project", 0, 3, 0), ("y_event", 3, 0), ("y_event", 3, 1), ("project_own", 3, 2),
    ("y_event", 4, 0), ("y_event", 4, 1), ("x_event", 2), ("project", 3, 2, 1), ("project_own", 5, 2),
    ("project_own", 7, 1), ("activate", 0, 3, 0), ("activate", 3, 2, 1), ("down", 2), ("weigh", 7), ("weigh", 5),
    ("weigh", 6), ("weigh", 3), ("weigh", 4), ("weigh", 1), ("weigh", 2), ("weigh", 0), ("x_event", 3),
    ("project", 5, 2, 2), ("x_event", 4), ("project", 7, 1, 3), ("activate", 5, 2, 2), ("activate", 7, 1, 3),
    ("down", 4), ("down", 3), ("down", 1), ("xb_event", 4, 0), ("xb_event", 4, 1), ("xb_event", 3, 0),
    ("xb_event", 3, 1), ("yb_event", 4, 0), ("yb_event", 4, 1), ("yb_event", 4, 2), ("yb_event", 4, 3),
    ("xb_event", 2, 0), ("xb_event", 2, 1), ("down", 0), ("xb_event", 1, 0), ("xb_event", 1, 1),
    ("yb_event", 3, 0), ("yb_event", 3, 1), ("yb_event", 3, 2), ("yb_event", 3, 3), ("xb_event", 0, 0),
    ("xb_event", 0, 1), ("yb_event", 2, 0), ("yb_event", 2, 1), ("yb_event", 2, 2), ("yb_event", 2, 3),
    ("yb_event", 0, 0), ("yb_event", 0, 1), ("yb_event", 0, 2), ("yb_event", 0, 3), ("yb_event", 1, 0),
    ("yb_event", 1, 1), ("yb_event", 1, 2), ("yb_event", 1, 3), ("finish", 0), ("finish", 1), ("finish", 2),
    ("finish", 3),
)


def kernel(
    routes_ref, gains_ref, hid, wg, wu, wd, out,
    meta, rows, x_all, y_out, w_gu, w_d, sel, mix, gu, gu_out, gu_in, act,
    own, other, x_in, q_out, back, z_out, z_in, fin, fin_in, residual,
    sent, ra, rm, rz, ry, rx, rp, rxb, ryb, rzb, rf, sl,
):
    g, a, e = lax.axis_index("grp"), lax.axis_index("attn"), lax.axis_index("exp")
    z, y = e // YS, e % YS
    h = g % 2
    half = own.shape[-1]

    def at_x(d):
        return ((g + d + GS) % GS, a, e)

    def at_zx(sign, d):
        return ((g + d) % GS, a, ((z + sign + ZS) % ZS) * YS + y)

    def at_y(d):
        return (g, a, z * YS + (y + d + YS) % YS)

    def at_z(d):
        return (g, a, ((z + d + ZS) % ZS) * YS + y)

    core = (g, 1 - a, e)

    def cols(c, base=0):
        first, size = PIECES[c]
        return pl.ds(base + first * 128, size * 128)

    def pair(c, base=0):
        first, size = PAIRS[c]
        return pl.ds(base + first * 128, size * 128)

    def send(src, dst, ss, rs, dev):
        pltpu.make_async_remote_copy(
            src_ref=src, dst_ref=dst, send_sem=sent.at[ss], recv_sem=rs, device_id=dev, device_id_type=MESH
        ).start()

    def await_all(ref, sem):
        pltpu.make_async_copy(ref, ref, sem).wait()

    peers = [at_x(d) for d in (1, 2, 3)] + [at_y(d) for d in (1, 2, 3)]
    peers += [at_z(r) for r in REL[1:]] + [core]
    peers += [at_zx(sign, d) for sign in (1, -1) for d in (1, 2, 3)]
    barrier = pltpu.get_barrier_semaphore()
    for dev in peers:
        pl.semaphore_signal(barrier, inc=1, device_id=dev, device_id_type=MESH)

    mine, theirs = h * half, (1 - h) * half
    def load(src, dst, sem):
        pltpu.make_async_copy(src, dst, sem).start()

    meta[0] = jnp.full(meta.shape[1:], -1.0, F32)
    for k in range(6):
        meta[0, k : k + 1, :SLAB] = routes_ref[k].astype(F32)
        meta[0, 8 + k : 9 + k, :SLAB] = gains_ref[k]

    my_rows = pl.ds(pl.multiple_of(g * 16, 16), 16)
    load(hid.at[:, pl.ds(pl.multiple_of(mine, 128), half)], rows.at[0, my_rows, :], sl.at[0])
    pl.semaphore_wait(barrier, len(peers))

    for c in CS:
        for sign, first in ((1, 3), (-1, 7), (0, -1)):
            for d in (1, 3, 2, 0) if sign else (1, 3, 2):
                there = ((g + d) % 2) * half + PIECES[c][0] * 128
                n = first + d
                send(
                    hid.at[:, pl.ds(pl.multiple_of(there, 128), PIECES[c][1] * 128)],
                    rows.at[AT[-sign], my_rows, cols(c)], 0, ra.at[c, abs(sign)], at_zx(sign, d),
                )
    for r in REL[1:]:
        back_at = AT[-r] if r != 4 else AT[4]
        send(meta.at[0], meta.at[back_at], 1, rm.at[0], at_z(r))
    for at, start in ((0, mine), (half, theirs)):
        there, here = pl.ds(pl.multiple_of(start, 128), half), pl.ds(at, half)
        load(wg.at[:, there], w_gu.at[pl.ds(0, wg.shape[0]), here], sl.at[1])
        load(wu.at[:, there], w_gu.at[pl.ds(wg.shape[0], wg.shape[0]), here], sl.at[1])
        load(wd.at[:, there], w_d.at[:, here], sl.at[2])
        load(hid.at[:, there], residual.at[:, here], sl.at[3])

    slots = YS * CAPS
    slot = lax.broadcasted_iota(jnp.int32, (slots, 128), 0)
    expert = (z * YS + (y + slot // CAPS) % YS).astype(F32)
    place = (lax.broadcasted_iota(jnp.int32, (slots, SLAB), 0) % CAPS).astype(F32)
    r_in = lax.broadcasted_iota(jnp.int32, (SLAB, SLAB), 0)
    r_out = lax.broadcasted_iota(jnp.int32, (SLAB, SLAB), 1)
    earlier = (r_in < r_out).astype(F32).astype(BF16)
    eye = (r_in == r_out).astype(F32).astype(BF16)

    def table(i):
        block = meta[i]
        picks = jnp.zeros((slots, 128), F32)
        for k in range(6):
            picks = jnp.where(block[k : k + 1, :] == expert, 1.0, picks)
        picks = picks[:, :SLAB]
        before = jnp.dot(picks.astype(BF16), earlier, preferred_element_type=F32)
        sel[i] = jnp.where(before == place, picks, 0.0).astype(BF16)

    def weigh(i):
        block = meta[i]
        gains = jnp.zeros((slots, 128), F32)
        for k in range(6):
            gains = jnp.where(block[k : k + 1, :] == expert, block[8 + k : 9 + k, :], gains)
        weighed = (sel[i].astype(F32) * gains[:, :SLAB]).astype(BF16)
        mix[i] = lax.dot_general(eye, weighed, NT, preferred_element_type=F32).astype(BF16)

    def z_send(s, c):
        for sign, k in WAYS:
            if s == 4 and FAR[c] != k:
                continue
            src = AT[-sign * (s - 1)]
            dst = AT[-sign * s] if s < 4 else AT[4]
            send(rows.at[src, :, cols(c)], rows.at[dst, :, cols(c)], 2, rz.at[c, s - 2], at_z(sign))

    def z_event(s, c):
        i0, n = SPAN[s]
        if s == 0:
            if c == 0:
                await_all(rows.at[0, my_rows, :], sl.at[0])
            await_all(rows.at[0, pl.ds(0, SLAB - 16), cols(c)], ra.at[c, 0])
        else:
            await_all(rows.at[pl.ds(i0, n), :, cols(c)], ra.at[c, 1] if s == 1 else rz.at[c, s - 2])
        if 1 <= s < 4:
            z_send(s + 1, c)

    def select(s, c):
        i0, n = SPAN[s]
        for i in range(i0, i0 + n):
            got = jnp.dot(sel[i], rows[i, :, pair(c)], preferred_element_type=F32).astype(BF16)
            x_all[i, 0, :, pair(c)] = got[0:CAPS]
            for d in (1, 2, 3):
                y_out[i, d - 1, :, pair(c)] = got[d * CAPS : (d + 1) * CAPS]
        for d in (1, 3, 2):
            send(
                y_out.at[pl.ds(i0, n), d - 1, :, pair(c)], x_all.at[pl.ds(i0, n), YS - d, :, pair(c)],
                3, ry.at[c, s], at_y(d),
            )

    def y_event(s, c):
        i0, n = SPAN[s]
        await_all(x_all.at[pl.ds(i0, n), pl.ds(1, 3), :, pair(c)], ry.at[c, s])
        for k, step in ((0, 1), (1, -1)):
            lines, blocks = (pl.ds(i0 + k, 1), pl.ds(0, YS)) if n == 2 else (pl.ds(i0, 1), pl.ds(2 * k, 2))
            send(
                x_all.at[lines, blocks, :, pair(c)], x_all.at[lines, blocks, :, pair(c, half)],
                4, rx.at[s], at_x(step),
            )

    def x_event(s):
        i0, n = SPAN[s]
        await_all(x_all.at[pl.ds(i0, n), :, :, pl.ds(half, half)], rx.at[s])

    def project_own(i0, n):
        block = x_all[pl.ds(i0, n), :, :, pl.ds(0, half)].reshape(n * SLAB, half)
        gu[pl.ds(i0 * SLAB, n * SLAB)] = lax.dot_general(block, w_gu[:, :half], NT, preferred_element_type=F32)

    def project(i0, n, number):
        at = pl.ds(i0 * SLAB, n * SLAB)
        block = x_all[pl.ds(i0, n), :, :, pl.ds(half, half)].reshape(n * SLAB, half)
        made = gu[at] + lax.dot_general(block, w_gu[:, half:], NT, preferred_element_type=F32)
        gu[at] = made
        gu_out[at] = made.astype(BF16)
        send(gu_out.at[at], gu_in.at[at], 5, rp.at[number], core)

    def activate(i0, n, number):
        at = pl.ds(i0 * SLAB, n * SLAB)
        await_all(gu_in.at[at], rp.at[number])
        total = gu[at] + gu_in[at].astype(F32)
        ff = total.shape[1] // 2
        gate, up = total[:, :ff], total[:, ff:]
        act[at] = (gate / (1.0 + jnp.exp(-gate)) * up).astype(BF16)

    def down(s):
        i0, n = SPAN[s]
        block = act[pl.ds(i0 * SLAB, n * SLAB)]
        for c in (0, 1):
            made = jnp.dot(block, w_d[:, pair(c, half)], preferred_element_type=F32).astype(BF16)
            other[pl.ds(i0, n), :, :, pair(c)] = made.reshape(n, YS, CAPS, made.shape[-1])
            for k, step in ((0, 1), (1, -1)):
                lines, blocks = (pl.ds(i0 + k, 1), pl.ds(0, YS)) if n == 2 else (pl.ds(i0, 1), pl.ds(2 * k, 2))
                send(
                    other.at[lines, blocks, :, pair(c)], x_in.at[lines, blocks, :, pair(c)],
                    6, rxb.at[c, s], at_x(step),
                )
        for c in (0, 1):
            made = jnp.dot(block, w_d[:, pair(c)], preferred_element_type=F32)
            own[pl.ds(i0, n), :, :, pair(c)] = made.reshape(n, YS, CAPS, made.shape[-1])

    def xb_event(s, c):
        i0, n = SPAN[s]
        at = pl.ds(i0, n)
        await_all(x_in.at[at, :, :, pair(c)], rxb.at[c, s])
        total = (own[at, :, :, pair(c)] + x_in[at, :, :, pair(c)].astype(F32)).astype(BF16)
        back[at, 0, :, pair(c)] = total[:, 0]
        for d in (1, 2, 3):
            q_out[at, d - 1, :, pair(c)] = total[:, d]
        for d in (1, 3, 2):
            send(
                q_out.at[at, d - 1, :, pair(c)], back.at[at, YS - d, :, pair(c)],
                7, ryb.at[c, s], at_y(d),
            )

    def yb_event(s, c):
        i0, n = SPAN[s]
        if c % 2 == 0:
            await_all(back.at[pl.ds(i0, n), pl.ds(1, 3), :, pair(c // 2)], ryb.at[c // 2, s])
        width = PIECES[c][1] * 128
        if s == 0:
            total = jnp.dot(mix[0], back[0, :, :, cols(c)].reshape(slots, width), preferred_element_type=F32)
            fin[:, cols(c)] = total.astype(BF16)
            spread(fin, c, 0, -1, (1, 3, 2))
            return
        first_way = FAR[c] if s == 3 else 0
        for sign, k in WAYS:
            if s == 4 and FAR[c] != k:
                continue
            i = AT[sign * s] if s < 4 else AT[4]
            total = jnp.dot(mix[i], back[i, :, :, cols(c)].reshape(slots, width), preferred_element_type=F32)
            if s < 3 or (s == 3 and FAR[c] == k):
                if k == first_way:
                    ways = pl.ds(0, 2) if s < 3 else pl.ds(k, 1)
                    await_all(z_in.at[ways, s - 1, :, cols(c)], rzb.at[c, s - 1])
                total = total + z_in[k, s - 1, :, cols(c)].astype(F32)
            z_out[k, s - 1, :, cols(c)] = total.astype(BF16)
            if s == 1:
                spread(z_out.at[k, 0], c, sign, 3 + 4 * k, (1, 3, 2, 0))
            else:
                send(
                    z_out.at[k, s - 1, :, cols(c)], z_in.at[k, s - 2, :, cols(c)],
                    8, rzb.at[c, s - 2], at_z(sign),
                )

    def spread(src, c, sign, first, far):
        for d in far:
            to_rows = pl.ds(pl.multiple_of(((g + d) % GS) * 16, 16), 16)
            n = first + d
            send(src.at[to_rows, cols(c)], fin_in.at[n, :, cols(c)], 9, rf.at[c], at_zx(sign, d))

    def tables():
        await_all(meta.at[pl.ds(1, ZS - 1)], rm.at[0])

    def loaded():
        for ref, n in ((w_gu, 1), (w_d, 2), (residual, 3)):
            await_all(ref, sl.at[n])

    def finish(c):
        await_all(fin_in.at[:, :, cols(c)], rf.at[c])
        here, there = cols(c), cols(c, half)
        moe = fin[my_rows, here].astype(F32)
        for n in (1, 3, 5, 7, 9):
            moe = moe + fin_in[n, :, here].astype(F32)
        first, size = PIECES[c]
        at = pl.ds(pl.multiple_of(mine + first * 128, 128), size * 128)
        out[:, at] = (residual[:, here].astype(F32) + moe).astype(BF16)
        moe = fin_in[0, :, here].astype(F32)
        for n in (2, 4, 6, 8, 10):
            moe = moe + fin_in[n, :, here].astype(F32)
        at = pl.ds(pl.multiple_of(theirs + first * 128, 128), size * 128)
        out[:, at] = (residual[:, there].astype(F32) + moe).astype(BF16)

    steps = dict(
        table=table, tables=tables, weigh=weigh, z_event=z_event, select=select, y_event=y_event, loaded=loaded, x_event=x_event,
        project_own=project_own, project=project, activate=activate, down=down, xb_event=xb_event, yb_event=yb_event, finish=finish,
    )
    for step, *given in ORDER:
        steps[step](*given)
    five = rows.at[pl.ds(0, 5)]
    sizes = (fin_in, meta.at[pl.ds(0, ZS - 1)], five, y_out, other, gu_out, other, q_out, five, fin_in)
    for n, ref in enumerate(sizes):
        await_all(ref, sent.at[n])


def body(hidden_rows, routes, route_gain, gate_weight, up_weight, down_weight):
    hid = hidden_rows[0]
    n, width = hid.shape
    ff = gate_weight.shape[1]
    half = width // 2
    picked, gains = (jnp.transpose(v, (2, 0, 1)) for v in (routes, route_gain))
    total, n_c = ZS * SLAB, len(PIECES)
    vmem = pltpu.VMEM
    dma = pltpu.SemaphoreType.DMA
    any_spec = pl.BlockSpec(memory_space=pl.ANY)
    out = pl.pallas_call(
        kernel,
        out_shape=pltpu.VMEM((n, width), BF16),
        in_specs=[pl.BlockSpec(memory_space=pltpu.VMEM)] * 2 + [any_spec] * 4,
        out_specs=pl.BlockSpec(memory_space=pltpu.VMEM),
        scratch_shapes=[
            vmem((ZS, 16, 128), F32),
            vmem((ZS, SLAB, half), BF16),
            vmem((ZS, YS, CAPS, width), BF16),
            vmem((ZS, 3, CAPS, half), BF16),
            vmem((2 * ff, width), BF16),
            vmem((ff, width), BF16),
            vmem((ZS, YS * CAPS, SLAB), BF16),
            vmem((ZS, SLAB, YS * CAPS), BF16),
            vmem((total, 2 * ff), F32),
            vmem((total, 2 * ff), BF16),
            vmem((total, 2 * ff), BF16),
            vmem((total, ff), BF16),
            vmem((ZS, YS, CAPS, half), F32),
            vmem((ZS, YS, CAPS, half), BF16),
            vmem((ZS, YS, CAPS, half), BF16),
            vmem((ZS, 3, CAPS, half), BF16),
            vmem((ZS, YS, CAPS, half), BF16),
            vmem((2, 4, SLAB, half), BF16),
            vmem((2, 3, SLAB, half), BF16),
            vmem((SLAB, half), BF16),
            vmem((11, 16, half), BF16),
            vmem((n, width), BF16),
            dma((10,)), dma((n_c, 2)), dma((1,)), dma((n_c, 3)), dma((2, 5)), dma((5,)), dma((4,)),
            dma((2, 5)), dma((2, 5)), dma((n_c, 3)), dma((n_c,)), dma((4,)),
        ],
        compiler_params=pltpu.CompilerParams(
            collective_id=0, has_side_effects=True, vmem_limit_bytes=60 * 1024 * 1024
        ),
        name="routed_layer",
    )(picked, gains, hid, gate_weight[0], up_weight[0], down_weight[0])
    return out[None]


def solution(mesh):
    placed = (
        P("exp", "grp", "attn"),
        P("exp", None, None),
        P("exp", None, None),
        P("exp", "grp", "attn"),
        P("exp", "grp", "attn"),
        P("exp", "grp", "attn"),
    )
    return jax.shard_map(
        body, mesh=mesh, in_specs=placed, out_specs=P("exp", "grp", "attn"), check_vma=False
    )
```

```python
import functools

import jax
import jax.numpy as jnp
from jax import lax
from jax.experimental import pallas as pl
from jax.experimental.pallas import tpu as pltpu
from jax.sharding import PartitionSpec as P

MESH = pl.DeviceIdType.MESH
NT = (((1,), (1,)), ((), ()))
F32, BF16 = jnp.float32, jnp.bfloat16

REL = (0, 1, -1, 2, -2, 3, -3, 4)
AT = {r: i for i, r in enumerate(REL)}
SPAN = ((0, 1), (1, 2), (3, 2), (5, 2), (7, 1))
ZS, YS, GS, CAPS, SLAB = 8, 4, 4, 16, 64
PIECES = ((0, 3), (3, 2), (5, 3), (8, 2))
FAR = (0, 1, 1, 0)
CS = range(len(PIECES))
PAIRS = ((0, 5), (5, 5))
WAYS = ((1, 0), (-1, 1))

ORDER = (
    ("table", 0), ("z_event", 0, 0), ("z_event", 0, 1), ("z_event", 0, 2), ("z_event", 0, 3), ("tables",),
    ("table", 1), ("table", 2), ("z_event", 1, 0), ("z_event", 1, 1), ("z_event", 1, 2), ("z_event", 1, 3),
    ("select", 0, 0), ("select", 0, 1), ("select", 1, 0), ("select", 1, 1), ("table", 3), ("table", 4),
    ("z_event", 2, 0), ("z_event", 2, 1), ("select", 2, 0), ("z_event", 2, 2), ("z_event", 2, 3), ("select", 2, 1),
    ("y_event", 0, 0), ("y_event", 0, 1), ("y_event", 1, 0), ("y_event", 1, 1), ("table", 5), ("table", 6),
    ("z_event", 3, 0), ("z_event", 3, 1), ("select", 3, 0), ("z_event", 3, 2), ("z_event", 3, 3), ("select", 3, 1),
    ("table", 7), ("y_event", 2, 0), ("y_event", 2, 1), ("loaded",), ("project_own", 0, 3), ("z_event", 4, 0),
    ("z_event", 4, 1), ("select", 4, 0), ("z_event", 4, 2), ("z_event", 4, 3), ("select", 4, 1), ("x_event", 0),
    ("x_event", 1), ("project", 0, 3, 0), ("y_event", 3, 0), ("y_event", 3, 1), ("project_own", 3, 2),
    ("y_event", 4, 0), ("y_event", 4, 1), ("x_event", 2), ("project", 3, 2, 1), ("project_own", 5, 2),
    ("project_own", 7, 1), ("activate", 0, 3, 0), ("activate", 3, 2, 1), ("down", 2), ("weigh", 7), ("weigh", 5),
    ("weigh", 6), ("weigh", 3), ("weigh", 4), ("weigh", 1), ("weigh", 2), ("weigh", 0), ("down_own", 2),
    ("x_event", 3), ("project", 5, 2, 2), ("x_event", 4), ("project", 7, 1, 3), ("activate", 5, 2, 2),
    ("activate", 7, 1, 3), ("down", 4), ("down", 3), ("down_own", 4), ("down_own", 3), ("down", 1),
    ("xb_event", 4, 0), ("xb_event", 4, 1), ("xb_event", 3, 0), ("xb_event", 3, 1), ("yb_event", 4, 0),
    ("yb_event", 4, 1), ("yb_event", 4, 2), ("yb_event", 4, 3), ("xb_event", 2, 0), ("xb_event", 2, 1),
    ("down", 0), ("down_own", 1), ("xb_event", 1, 0), ("xb_event", 1, 1), ("yb_event", 3, 0), ("yb_event", 3, 1),
    ("yb_event", 3, 2), ("yb_event", 3, 3), ("down_own", 0), ("xb_event", 0, 0), ("xb_event", 0, 1),
    ("yb_event", 2, 0), ("yb_event", 2, 1), ("yb_event", 2, 2), ("yb_event", 2, 3), ("yb_event", 0, 0),
    ("yb_event", 0, 1), ("yb_event", 0, 2), ("yb_event", 0, 3), ("yb_event", 1, 0), ("yb_event", 1, 1),
    ("yb_event", 1, 2), ("yb_event", 1, 3), ("finish", 0), ("finish", 1), ("finish", 2), ("finish", 3),
)


def kernel(
    routes_ref, gains_ref, hid, wg, wu, wd, out,
    meta, rows, x_all, y_out, w_gu, w_d, sel, mix, gu, gu_out, gu_in, act,
    own, other, x_in, q_out, back, z_out, z_in, fin, fin_in, residual,
    sent, ra, rm, rz, ry, rx, rp, rxb, ryb, rzb, rf, sl,
):
    g, a, e = lax.axis_index("grp"), lax.axis_index("attn"), lax.axis_index("exp")
    z, y = e // YS, e % YS
    h = g % 2
    half = own.shape[-1]

    def at_x(d):
        return ((g + d + GS) % GS, a, e)

    def at_zx(sign, d):
        return ((g + d) % GS, a, ((z + sign + ZS) % ZS) * YS + y)

    def at_y(d):
        return (g, a, z * YS + (y + d + YS) % YS)

    def at_z(d):
        return (g, a, ((z + d + ZS) % ZS) * YS + y)

    core = (g, 1 - a, e)

    def cols(c, base=0):
        first, size = PIECES[c]
        return pl.ds(base + first * 128, size * 128)

    def pair(c, base=0):
        first, size = PAIRS[c]
        return pl.ds(base + first * 128, size * 128)

    def send(src, dst, ss, rs, dev):
        pltpu.make_async_remote_copy(
            src_ref=src, dst_ref=dst, send_sem=sent.at[ss], recv_sem=rs, device_id=dev, device_id_type=MESH
        ).start()

    def await_all(ref, sem):
        pltpu.make_async_copy(ref, ref, sem).wait()

    peers = [at_x(d) for d in (1, 2, 3)] + [at_y(d) for d in (1, 2, 3)]
    peers += [at_z(r) for r in REL[1:]] + [core]
    peers += [at_zx(sign, d) for sign in (1, -1) for d in (1, 2, 3)]
    barrier = pltpu.get_barrier_semaphore()
    for dev in peers:
        pl.semaphore_signal(barrier, inc=1, device_id=dev, device_id_type=MESH)

    mine, theirs = h * half, (1 - h) * half
    def load(src, dst, sem):
        pltpu.make_async_copy(src, dst, sem).start()

    meta[0] = jnp.full(meta.shape[1:], -1.0, F32)
    for k in range(6):
        meta[0, k : k + 1, :SLAB] = routes_ref[k].astype(F32)
        meta[0, 8 + k : 9 + k, :SLAB] = gains_ref[k]

    my_rows = pl.ds(pl.multiple_of(g * 16, 16), 16)
    load(hid.at[:, pl.ds(pl.multiple_of(mine, 128), half)], rows.at[0, my_rows, :], sl.at[0])
    pl.semaphore_wait(barrier, len(peers))

    for c in CS:
        for sign, first in ((1, 3), (-1, 7), (0, -1)):
            for d in (1, 3, 2, 0) if sign else (1, 3, 2):
                there = ((g + d) % 2) * half + PIECES[c][0] * 128
                n = first + d
                send(
                    hid.at[:, pl.ds(pl.multiple_of(there, 128), PIECES[c][1] * 128)],
                    rows.at[AT[-sign], my_rows, cols(c)], 0, ra.at[c, abs(sign)], at_zx(sign, d),
                )
    for r in REL[1:]:
        back_at = AT[-r] if r != 4 else AT[4]
        send(meta.at[0], meta.at[back_at], 1, rm.at[0], at_z(r))
    for at, start in ((0, mine), (half, theirs)):
        there, here = pl.ds(pl.multiple_of(start, 128), half), pl.ds(at, half)
        load(wg.at[:, there], w_gu.at[pl.ds(0, wg.shape[0]), here], sl.at[1])
        load(wu.at[:, there], w_gu.at[pl.ds(wg.shape[0], wg.shape[0]), here], sl.at[1])
        load(wd.at[:, there], w_d.at[:, here], sl.at[2])
        load(hid.at[:, there], residual.at[:, here], sl.at[3])

    slots = YS * CAPS
    slot = lax.broadcasted_iota(jnp.int32, (slots, 128), 0)
    expert = (z * YS + (y + slot // CAPS) % YS).astype(F32)
    place = (lax.broadcasted_iota(jnp.int32, (slots, SLAB), 0) % CAPS).astype(F32)
    r_in = lax.broadcasted_iota(jnp.int32, (SLAB, SLAB), 0)
    r_out = lax.broadcasted_iota(jnp.int32, (SLAB, SLAB), 1)
    earlier = (r_in < r_out).astype(F32).astype(BF16)
    eye = (r_in == r_out).astype(F32).astype(BF16)

    def table(i):
        block = meta[i]
        picks = jnp.zeros((slots, 128), F32)
        for k in range(6):
            picks = jnp.where(block[k : k + 1, :] == expert, 1.0, picks)
        picks = picks[:, :SLAB]
        before = jnp.dot(picks.astype(BF16), earlier, preferred_element_type=F32)
        sel[i] = jnp.where(before == place, picks, 0.0).astype(BF16)

    def weigh(i):
        block = meta[i]
        gains = jnp.zeros((slots, 128), F32)
        for k in range(6):
            gains = jnp.where(block[k : k + 1, :] == expert, block[8 + k : 9 + k, :], gains)
        weighed = (sel[i].astype(F32) * gains[:, :SLAB]).astype(BF16)
        mix[i] = lax.dot_general(eye, weighed, NT, preferred_element_type=F32).astype(BF16)

    def z_send(s, c):
        for sign, k in WAYS:
            if s == 4 and FAR[c] != k:
                continue
            src = AT[-sign * (s - 1)]
            dst = AT[-sign * s] if s < 4 else AT[4]
            send(rows.at[src, :, cols(c)], rows.at[dst, :, cols(c)], 2, rz.at[c, s - 2], at_z(sign))

    def z_event(s, c):
        i0, n = SPAN[s]
        if s == 0:
            if c == 0:
                await_all(rows.at[0, my_rows, :], sl.at[0])
            await_all(rows.at[0, pl.ds(0, SLAB - 16), cols(c)], ra.at[c, 0])
        else:
            await_all(rows.at[pl.ds(i0, n), :, cols(c)], ra.at[c, 1] if s == 1 else rz.at[c, s - 2])
        if 1 <= s < 4:
            z_send(s + 1, c)

    def select(s, c):
        i0, n = SPAN[s]
        for i in range(i0, i0 + n):
            got = jnp.dot(sel[i], rows[i, :, pair(c)], preferred_element_type=F32).astype(BF16)
            x_all[i, 0, :, pair(c)] = got[0:CAPS]
            for d in (1, 2, 3):
                y_out[i, d - 1, :, pair(c)] = got[d * CAPS : (d + 1) * CAPS]
        for d in (1, 3, 2):
            send(
                y_out.at[pl.ds(i0, n), d - 1, :, pair(c)], x_all.at[pl.ds(i0, n), YS - d, :, pair(c)],
                3, ry.at[c, s], at_y(d),
            )

    def y_event(s, c):
        i0, n = SPAN[s]
        await_all(x_all.at[pl.ds(i0, n), pl.ds(1, 3), :, pair(c)], ry.at[c, s])
        for k, step in ((0, 1), (1, -1)):
            lines, blocks = (pl.ds(i0 + k, 1), pl.ds(0, YS)) if n == 2 else (pl.ds(i0, 1), pl.ds(2 * k, 2))
            send(
                x_all.at[lines, blocks, :, pair(c)], x_all.at[lines, blocks, :, pair(c, half)],
                4, rx.at[s], at_x(step),
            )

    def x_event(s):
        i0, n = SPAN[s]
        await_all(x_all.at[pl.ds(i0, n), :, :, pl.ds(half, half)], rx.at[s])

    def project_own(i0, n):
        block = x_all[pl.ds(i0, n), :, :, pl.ds(0, half)].reshape(n * SLAB, half)
        gu[pl.ds(i0 * SLAB, n * SLAB)] = lax.dot_general(block, w_gu[:, :half], NT, preferred_element_type=F32)

    def project(i0, n, number):
        at = pl.ds(i0 * SLAB, n * SLAB)
        block = x_all[pl.ds(i0, n), :, :, pl.ds(half, half)].reshape(n * SLAB, half)
        made = gu[at] + lax.dot_general(block, w_gu[:, half:], NT, preferred_element_type=F32)
        gu[at] = made
        gu_out[at] = made.astype(BF16)
        send(gu_out.at[at], gu_in.at[at], 5, rp.at[number], core)

    def activate(i0, n, number):
        at = pl.ds(i0 * SLAB, n * SLAB)
        await_all(gu_in.at[at], rp.at[number])
        total = gu[at] + gu_in[at].astype(F32)
        ff = total.shape[1] // 2
        gate, up = total[:, :ff], total[:, ff:]
        act[at] = (gate / (1.0 + jnp.exp(-gate)) * up).astype(BF16)

    def down(s):
        i0, n = SPAN[s]
        block = act[pl.ds(i0 * SLAB, n * SLAB)]
        for c in (0, 1):
            made = jnp.dot(block, w_d[:, pair(c, half)], preferred_element_type=F32).astype(BF16)
            other[pl.ds(i0, n), :, :, pair(c)] = made.reshape(n, YS, CAPS, made.shape[-1])
            for k, step in ((0, 1), (1, -1)):
                lines, blocks = (pl.ds(i0 + k, 1), pl.ds(0, YS)) if n == 2 else (pl.ds(i0, 1), pl.ds(2 * k, 2))
                send(
                    other.at[lines, blocks, :, pair(c)], x_in.at[lines, blocks, :, pair(c)],
                    6, rxb.at[c, s], at_x(step),
                )

    def down_own(s):
        i0, n = SPAN[s]
        block = act[pl.ds(i0 * SLAB, n * SLAB)]
        for c in (0, 1):
            made = jnp.dot(block, w_d[:, pair(c)], preferred_element_type=F32)
            own[pl.ds(i0, n), :, :, pair(c)] = made.reshape(n, YS, CAPS, made.shape[-1])

    def xb_event(s, c):
        i0, n = SPAN[s]
        at = pl.ds(i0, n)
        await_all(x_in.at[at, :, :, pair(c)], rxb.at[c, s])
        total = (own[at, :, :, pair(c)] + x_in[at, :, :, pair(c)].astype(F32)).astype(BF16)
        back[at, 0, :, pair(c)] = total[:, 0]
        for d in (1, 2, 3):
            q_out[at, d - 1, :, pair(c)] = total[:, d]
        for d in (1, 3, 2):
            send(
                q_out.at[at, d - 1, :, pair(c)], back.at[at, YS - d, :, pair(c)],
                7, ryb.at[c, s], at_y(d),
            )

    def yb_event(s, c):
        i0, n = SPAN[s]
        if c % 2 == 0:
            await_all(back.at[pl.ds(i0, n), pl.ds(1, 3), :, pair(c // 2)], ryb.at[c // 2, s])
        width = PIECES[c][1] * 128
        if s == 0:
            total = jnp.dot(mix[0], back[0, :, :, cols(c)].reshape(slots, width), preferred_element_type=F32)
            fin[:, cols(c)] = total.astype(BF16)
            spread(fin, c, 0, -1, (1, 3, 2))
            return
        first_way = FAR[c] if s == 3 else 0
        for sign, k in WAYS:
            if s == 4 and FAR[c] != k:
                continue
            i = AT[sign * s] if s < 4 else AT[4]
            total = jnp.dot(mix[i], back[i, :, :, cols(c)].reshape(slots, width), preferred_element_type=F32)
            if s < 3 or (s == 3 and FAR[c] == k):
                if k == first_way:
                    ways = pl.ds(0, 2) if s < 3 else pl.ds(k, 1)
                    await_all(z_in.at[ways, s - 1, :, cols(c)], rzb.at[c, s - 1])
                total = total + z_in[k, s - 1, :, cols(c)].astype(F32)
            z_out[k, s - 1, :, cols(c)] = total.astype(BF16)
            if s == 1:
                spread(z_out.at[k, 0], c, sign, 3 + 4 * k, (1, 3, 2, 0))
            else:
                send(
                    z_out.at[k, s - 1, :, cols(c)], z_in.at[k, s - 2, :, cols(c)],
                    8, rzb.at[c, s - 2], at_z(sign),
                )

    def spread(src, c, sign, first, far):
        for d in far:
            to_rows = pl.ds(pl.multiple_of(((g + d) % GS) * 16, 16), 16)
            n = first + d
            send(src.at[to_rows, cols(c)], fin_in.at[n, :, cols(c)], 9, rf.at[c], at_zx(sign, d))

    def tables():
        await_all(meta.at[pl.ds(1, ZS - 1)], rm.at[0])

    def loaded():
        for ref, n in ((w_gu, 1), (w_d, 2), (residual, 3)):
            await_all(ref, sl.at[n])

    def finish(c):
        await_all(fin_in.at[:, :, cols(c)], rf.at[c])
        here, there = cols(c), cols(c, half)
        moe = fin[my_rows, here].astype(F32)
        for n in (1, 3, 5, 7, 9):
            moe = moe + fin_in[n, :, here].astype(F32)
        first, size = PIECES[c]
        at = pl.ds(pl.multiple_of(mine + first * 128, 128), size * 128)
        out[:, at] = (residual[:, here].astype(F32) + moe).astype(BF16)
        moe = fin_in[0, :, here].astype(F32)
        for n in (2, 4, 6, 8, 10):
            moe = moe + fin_in[n, :, here].astype(F32)
        at = pl.ds(pl.multiple_of(theirs + first * 128, 128), size * 128)
        out[:, at] = (residual[:, there].astype(F32) + moe).astype(BF16)

    steps = dict(
        table=table, tables=tables, weigh=weigh, z_event=z_event, select=select, y_event=y_event, loaded=loaded, x_event=x_event,
        project_own=project_own, project=project, activate=activate, down=down, down_own=down_own, xb_event=xb_event, yb_event=yb_event, finish=finish,
    )
    for step, *given in ORDER:
        steps[step](*given)
    five = rows.at[pl.ds(0, 5)]
    sizes = (fin_in, meta.at[pl.ds(0, ZS - 1)], five, y_out, other, gu_out, other, q_out, five, fin_in)
    for n, ref in enumerate(sizes):
        await_all(ref, sent.at[n])


def body(hidden_rows, routes, route_gain, gate_weight, up_weight, down_weight):
    hid = hidden_rows[0]
    n, width = hid.shape
    ff = gate_weight.shape[1]
    half = width // 2
    picked, gains = (jnp.transpose(v, (2, 0, 1)) for v in (routes, route_gain))
    total, n_c = ZS * SLAB, len(PIECES)
    vmem = pltpu.VMEM
    dma = pltpu.SemaphoreType.DMA
    any_spec = pl.BlockSpec(memory_space=pl.ANY)
    out = pl.pallas_call(
        kernel,
        out_shape=pltpu.VMEM((n, width), BF16),
        in_specs=[pl.BlockSpec(memory_space=pltpu.VMEM)] * 2 + [any_spec] * 4,
        out_specs=pl.BlockSpec(memory_space=pltpu.VMEM),
        scratch_shapes=[
            vmem((ZS, 16, 128), F32),
            vmem((ZS, SLAB, half), BF16),
            vmem((ZS, YS, CAPS, width), BF16),
            vmem((ZS, 3, CAPS, half), BF16),
            vmem((2 * ff, width), BF16),
            vmem((ff, width), BF16),
            vmem((ZS, YS * CAPS, SLAB), BF16),
            vmem((ZS, SLAB, YS * CAPS), BF16),
            vmem((total, 2 * ff), F32),
            vmem((total, 2 * ff), BF16),
            vmem((total, 2 * ff), BF16),
            vmem((total, ff), BF16),
            vmem((ZS, YS, CAPS, half), F32),
            vmem((ZS, YS, CAPS, half), BF16),
            vmem((ZS, YS, CAPS, half), BF16),
            vmem((ZS, 3, CAPS, half), BF16),
            vmem((ZS, YS, CAPS, half), BF16),
            vmem((2, 4, SLAB, half), BF16),
            vmem((2, 3, SLAB, half), BF16),
            vmem((SLAB, half), BF16),
            vmem((11, 16, half), BF16),
            vmem((n, width), BF16),
            dma((10,)), dma((n_c, 2)), dma((1,)), dma((n_c, 3)), dma((2, 5)), dma((5,)), dma((4,)),
            dma((2, 5)), dma((2, 5)), dma((n_c, 3)), dma((n_c,)), dma((4,)),
        ],
        compiler_params=pltpu.CompilerParams(
            collective_id=0, has_side_effects=True, vmem_limit_bytes=60 * 1024 * 1024
        ),
        name="routed_layer",
    )(picked, gains, hid, gate_weight[0], up_weight[0], down_weight[0])
    return out[None]


def solution(mesh):
    placed = (
        P("exp", "grp", "attn"),
        P("exp", None, None),
        P("exp", None, None),
        P("exp", "grp", "attn"),
        P("exp", "grp", "attn"),
        P("exp", "grp", "attn"),
    )
    return jax.shard_map(
        body, mesh=mesh, in_specs=placed, out_specs=P("exp", "grp", "attn"), check_vma=False
    )
```

```python
import functools

import jax
import jax.numpy as jnp
from jax import lax
from jax.experimental import pallas as pl
from jax.experimental.pallas import tpu as pltpu
from jax.sharding import PartitionSpec as P

MESH = pl.DeviceIdType.MESH
NT = (((1,), (1,)), ((), ()))
F32, BF16 = jnp.float32, jnp.bfloat16

REL = (0, 1, -1, 2, -2, 3, -3, 4)
AT = {r: i for i, r in enumerate(REL)}
SPAN = ((0, 1), (1, 2), (3, 2), (5, 2), (7, 1))
ZS, YS, GS, CAPS, SLAB = 8, 4, 4, 16, 64
PIECES = ((0, 3), (3, 2), (5, 3), (8, 2))
FAR = (0, 1, 1, 0)
CS = range(len(PIECES))
PAIRS = ((0, 5), (5, 5))
WAYS = ((1, 0), (-1, 1))

ORDER = (
    ("table", 0), ("z_event", 0, 0), ("z_event", 0, 1), ("z_event", 0, 2), ("z_event", 0, 3), ("tables",),
    ("table", 1), ("table", 2), ("z_event", 1, 0), ("z_event", 1, 1), ("z_event", 1, 2), ("z_event", 1, 3),
    ("select", 0, 0), ("select", 0, 1), ("select", 1, 0), ("select", 1, 1), ("table", 3), ("table", 4),
    ("z_event", 2, 0), ("z_event", 2, 1), ("select", 2, 0), ("z_event", 2, 2), ("z_event", 2, 3), ("select", 2, 1),
    ("y_event", 0, 0), ("y_event", 0, 1), ("y_event", 1, 0), ("y_event", 1, 1), ("table", 5), ("table", 6),
    ("z_event", 3, 0), ("z_event", 3, 1), ("select", 3, 0), ("z_event", 3, 2), ("z_event", 3, 3), ("select", 3, 1),
    ("table", 7), ("y_event", 2, 0), ("y_event", 2, 1), ("loaded",), ("project_own", 0, 3), ("z_event", 4, 0),
    ("z_event", 4, 1), ("select", 4, 0), ("z_event", 4, 2), ("z_event", 4, 3), ("select", 4, 1), ("x_event", 0),
    ("x_event", 1), ("project", 0, 3, 0), ("y_event", 3, 0), ("y_event", 3, 1), ("project_own", 3, 2),
    ("y_event", 4, 0), ("y_event", 4, 1), ("x_event", 2), ("project", 3, 2, 1), ("project_own", 5, 2),
    ("project_own", 7, 1), ("activate", 0, 3, 0), ("activate", 3, 2, 1), ("down", 2), ("weigh", 7), ("weigh", 5),
    ("weigh", 6), ("weigh", 3), ("weigh", 4), ("weigh", 1), ("weigh", 2), ("weigh", 0), ("down_own", 2),
    ("x_event", 3), ("project", 5, 2, 2), ("x_event", 4), ("project", 7, 1, 3), ("activate", 5, 2, 2),
    ("activate", 7, 1, 3), ("down", 4), ("down", 3), ("down_own", 4), ("down_own", 3), ("down", 1),
    ("xb_event", 4, 0), ("xb_event", 4, 1), ("xb_event", 4, 2), ("xb_event", 4, 3), ("xb_event", 3, 0),
    ("xb_event", 3, 1), ("xb_event", 3, 2), ("xb_event", 3, 3), ("yb_event", 4, 0), ("yb_event", 4, 1),
    ("yb_event", 4, 2), ("yb_event", 4, 3), ("xb_event", 2, 0), ("xb_event", 2, 1), ("xb_event", 2, 2),
    ("xb_event", 2, 3), ("down", 0), ("down_own", 1), ("xb_event", 1, 0), ("xb_event", 1, 1), ("xb_event", 1, 2),
    ("xb_event", 1, 3), ("yb_event", 3, 0), ("yb_event", 3, 1), ("yb_event", 3, 2), ("yb_event", 3, 3),
    ("down_own", 0), ("xb_event", 0, 0), ("xb_event", 0, 1), ("xb_event", 0, 2), ("xb_event", 0, 3),
    ("yb_event", 2, 0), ("yb_event", 2, 1), ("yb_event", 2, 2), ("yb_event", 2, 3), ("yb_event", 0, 0),
    ("yb_event", 0, 1), ("yb_event", 0, 2), ("yb_event", 0, 3), ("yb_event", 1, 0), ("yb_event", 1, 1),
    ("yb_event", 1, 2), ("yb_event", 1, 3), ("finish", 0), ("finish", 1), ("finish", 2), ("finish", 3),
)


def kernel(
    routes_ref, gains_ref, hid, wg, wu, wd, out,
    meta, rows, x_all, y_out, w_gu, w_d, sel, mix, gu, gu_out, gu_in, act,
    own, other, x_in, q_out, back, z_out, z_in, fin, fin_in, residual,
    sent, ra, rm, rz, ry, rx, rp, rxb, ryb, rzb, rf, sl,
):
    g, a, e = lax.axis_index("grp"), lax.axis_index("attn"), lax.axis_index("exp")
    z, y = e // YS, e % YS
    h = g % 2
    half = own.shape[-1]

    def at_x(d):
        return ((g + d + GS) % GS, a, e)

    def at_zx(sign, d):
        return ((g + d) % GS, a, ((z + sign + ZS) % ZS) * YS + y)

    def at_y(d):
        return (g, a, z * YS + (y + d + YS) % YS)

    def at_z(d):
        return (g, a, ((z + d + ZS) % ZS) * YS + y)

    core = (g, 1 - a, e)

    def cols(c, base=0):
        first, size = PIECES[c]
        return pl.ds(base + first * 128, size * 128)

    def pair(c, base=0):
        first, size = PAIRS[c]
        return pl.ds(base + first * 128, size * 128)

    def send(src, dst, ss, rs, dev):
        pltpu.make_async_remote_copy(
            src_ref=src, dst_ref=dst, send_sem=sent.at[ss], recv_sem=rs, device_id=dev, device_id_type=MESH
        ).start()

    def await_all(ref, sem):
        pltpu.make_async_copy(ref, ref, sem).wait()

    peers = [at_x(d) for d in (1, 2, 3)] + [at_y(d) for d in (1, 2, 3)]
    peers += [at_z(r) for r in REL[1:]] + [core]
    peers += [at_zx(sign, d) for sign in (1, -1) for d in (1, 2, 3)]
    barrier = pltpu.get_barrier_semaphore()
    for dev in peers:
        pl.semaphore_signal(barrier, inc=1, device_id=dev, device_id_type=MESH)

    mine, theirs = h * half, (1 - h) * half
    def load(src, dst, sem):
        pltpu.make_async_copy(src, dst, sem).start()

    meta[0] = jnp.full(meta.shape[1:], -1.0, F32)
    for k in range(6):
        meta[0, k : k + 1, :SLAB] = routes_ref[k].astype(F32)
        meta[0, 8 + k : 9 + k, :SLAB] = gains_ref[k]

    my_rows = pl.ds(pl.multiple_of(g * 16, 16), 16)
    load(hid.at[:, pl.ds(pl.multiple_of(mine, 128), half)], rows.at[0, my_rows, :], sl.at[0])
    pl.semaphore_wait(barrier, len(peers))

    for c in CS:
        for sign, first in ((1, 3), (-1, 7), (0, -1)):
            for d in (1, 3, 2, 0) if sign else (1, 3, 2):
                there = ((g + d) % 2) * half + PIECES[c][0] * 128
                n = first + d
                send(
                    hid.at[:, pl.ds(pl.multiple_of(there, 128), PIECES[c][1] * 128)],
                    rows.at[AT[-sign], my_rows, cols(c)], 0, ra.at[c, abs(sign)], at_zx(sign, d),
                )
    for r in REL[1:]:
        back_at = AT[-r] if r != 4 else AT[4]
        send(meta.at[0], meta.at[back_at], 1, rm.at[0], at_z(r))
    for at, start in ((0, mine), (half, theirs)):
        there, here = pl.ds(pl.multiple_of(start, 128), half), pl.ds(at, half)
        load(wg.at[:, there], w_gu.at[pl.ds(0, wg.shape[0]), here], sl.at[1])
        load(wu.at[:, there], w_gu.at[pl.ds(wg.shape[0], wg.shape[0]), here], sl.at[1])
        load(wd.at[:, there], w_d.at[:, here], sl.at[2])
        load(hid.at[:, there], residual.at[:, here], sl.at[3])

    slots = YS * CAPS
    slot = lax.broadcasted_iota(jnp.int32, (slots, 128), 0)
    expert = (z * YS + (y + slot // CAPS) % YS).astype(F32)
    place = (lax.broadcasted_iota(jnp.int32, (slots, SLAB), 0) % CAPS).astype(F32)
    r_in = lax.broadcasted_iota(jnp.int32, (SLAB, SLAB), 0)
    r_out = lax.broadcasted_iota(jnp.int32, (SLAB, SLAB), 1)
    earlier = (r_in < r_out).astype(F32).astype(BF16)
    eye = (r_in == r_out).astype(F32).astype(BF16)

    def table(i):
        block = meta[i]
        picks = jnp.zeros((slots, 128), F32)
        for k in range(6):
            picks = jnp.where(block[k : k + 1, :] == expert, 1.0, picks)
        picks = picks[:, :SLAB]
        before = jnp.dot(picks.astype(BF16), earlier, preferred_element_type=F32)
        sel[i] = jnp.where(before == place, picks, 0.0).astype(BF16)

    def weigh(i):
        block = meta[i]
        gains = jnp.zeros((slots, 128), F32)
        for k in range(6):
            gains = jnp.where(block[k : k + 1, :] == expert, block[8 + k : 9 + k, :], gains)
        weighed = (sel[i].astype(F32) * gains[:, :SLAB]).astype(BF16)
        mix[i] = lax.dot_general(eye, weighed, NT, preferred_element_type=F32).astype(BF16)

    def z_send(s, c):
        for sign, k in WAYS:
            if s == 4 and FAR[c] != k:
                continue
            src = AT[-sign * (s - 1)]
            dst = AT[-sign * s] if s < 4 else AT[4]
            send(rows.at[src, :, cols(c)], rows.at[dst, :, cols(c)], 2, rz.at[c, s - 2], at_z(sign))

    def z_event(s, c):
        i0, n = SPAN[s]
        if s == 0:
            if c == 0:
                await_all(rows.at[0, my_rows, :], sl.at[0])
            await_all(rows.at[0, pl.ds(0, SLAB - 16), cols(c)], ra.at[c, 0])
        else:
            await_all(rows.at[pl.ds(i0, n), :, cols(c)], ra.at[c, 1] if s == 1 else rz.at[c, s - 2])
        if 1 <= s < 4:
            z_send(s + 1, c)

    def select(s, c):
        i0, n = SPAN[s]
        for i in range(i0, i0 + n):
            got = jnp.dot(sel[i], rows[i, :, pair(c)], preferred_element_type=F32).astype(BF16)
            x_all[i, 0, :, pair(c)] = got[0:CAPS]
            for d in (1, 2, 3):
                y_out[i, d - 1, :, pair(c)] = got[d * CAPS : (d + 1) * CAPS]
        for d in (1, 3, 2):
            send(
                y_out.at[pl.ds(i0, n), d - 1, :, pair(c)], x_all.at[pl.ds(i0, n), YS - d, :, pair(c)],
                3, ry.at[c, s], at_y(d),
            )

    def y_event(s, c):
        i0, n = SPAN[s]
        await_all(x_all.at[pl.ds(i0, n), pl.ds(1, 3), :, pair(c)], ry.at[c, s])
        for k, step in ((0, 1), (1, -1)):
            lines, blocks = (pl.ds(i0 + k, 1), pl.ds(0, YS)) if n == 2 else (pl.ds(i0, 1), pl.ds(2 * k, 2))
            send(
                x_all.at[lines, blocks, :, pair(c)], x_all.at[lines, blocks, :, pair(c, half)],
                4, rx.at[s], at_x(step),
            )

    def x_event(s):
        i0, n = SPAN[s]
        await_all(x_all.at[pl.ds(i0, n), :, :, pl.ds(half, half)], rx.at[s])

    def project_own(i0, n):
        block = x_all[pl.ds(i0, n), :, :, pl.ds(0, half)].reshape(n * SLAB, half)
        gu[pl.ds(i0 * SLAB, n * SLAB)] = lax.dot_general(block, w_gu[:, :half], NT, preferred_element_type=F32)

    def project(i0, n, number):
        at = pl.ds(i0 * SLAB, n * SLAB)
        block = x_all[pl.ds(i0, n), :, :, pl.ds(half, half)].reshape(n * SLAB, half)
        made = gu[at] + lax.dot_general(block, w_gu[:, half:], NT, preferred_element_type=F32)
        gu[at] = made
        gu_out[at] = made.astype(BF16)
        send(gu_out.at[at], gu_in.at[at], 5, rp.at[number], core)

    def activate(i0, n, number):
        at = pl.ds(i0 * SLAB, n * SLAB)
        await_all(gu_in.at[at], rp.at[number])
        total = gu[at] + gu_in[at].astype(F32)
        ff = total.shape[1] // 2
        gate, up = total[:, :ff], total[:, ff:]
        act[at] = (gate / (1.0 + jnp.exp(-gate)) * up).astype(BF16)

    def down(s):
        i0, n = SPAN[s]
        block = act[pl.ds(i0 * SLAB, n * SLAB)]
        for c in CS:
            made = jnp.dot(block, w_d[:, cols(c, half)], preferred_element_type=F32).astype(BF16)
            other[pl.ds(i0, n), :, :, cols(c)] = made.reshape(n, YS, CAPS, made.shape[-1])
            for k, step in ((0, 1), (1, -1)):
                lines, blocks = (pl.ds(i0 + k, 1), pl.ds(0, YS)) if n == 2 else (pl.ds(i0, 1), pl.ds(2 * k, 2))
                send(
                    other.at[lines, blocks, :, cols(c)], x_in.at[lines, blocks, :, cols(c)],
                    6, rxb.at[c, s], at_x(step),
                )

    def down_own(s):
        i0, n = SPAN[s]
        block = act[pl.ds(i0 * SLAB, n * SLAB)]
        for c in (0, 1):
            made = jnp.dot(block, w_d[:, pair(c)], preferred_element_type=F32)
            own[pl.ds(i0, n), :, :, pair(c)] = made.reshape(n, YS, CAPS, made.shape[-1])

    def xb_event(s, c):
        i0, n = SPAN[s]
        at = pl.ds(i0, n)
        await_all(x_in.at[at, :, :, cols(c)], rxb.at[c, s])
        total = (own[at, :, :, cols(c)] + x_in[at, :, :, cols(c)].astype(F32)).astype(BF16)
        back[at, 0, :, cols(c)] = total[:, 0]
        for d in (1, 2, 3):
            q_out[at, d - 1, :, cols(c)] = total[:, d]
        for d in (1, 3, 2):
            send(
                q_out.at[at, d - 1, :, cols(c)], back.at[at, YS - d, :, cols(c)],
                7, ryb.at[c, s], at_y(d),
            )

    def yb_event(s, c):
        i0, n = SPAN[s]
        await_all(back.at[pl.ds(i0, n), pl.ds(1, 3), :, cols(c)], ryb.at[c, s])
        width = PIECES[c][1] * 128
        if s == 0:
            total = jnp.dot(mix[0], back[0, :, :, cols(c)].reshape(slots, width), preferred_element_type=F32)
            fin[:, cols(c)] = total.astype(BF16)
            spread(fin, c, 0, -1, (1, 3, 2))
            return
        first_way = FAR[c] if s == 3 else 0
        for sign, k in WAYS:
            if s == 4 and FAR[c] != k:
                continue
            i = AT[sign * s] if s < 4 else AT[4]
            total = jnp.dot(mix[i], back[i, :, :, cols(c)].reshape(slots, width), preferred_element_type=F32)
            if s < 3 or (s == 3 and FAR[c] == k):
                if k == first_way:
                    ways = pl.ds(0, 2) if s < 3 else pl.ds(k, 1)
                    await_all(z_in.at[ways, s - 1, :, cols(c)], rzb.at[c, s - 1])
                total = total + z_in[k, s - 1, :, cols(c)].astype(F32)
            z_out[k, s - 1, :, cols(c)] = total.astype(BF16)
            if s == 1:
                spread(z_out.at[k, 0], c, sign, 3 + 4 * k, (1, 3, 2, 0))
            else:
                send(
                    z_out.at[k, s - 1, :, cols(c)], z_in.at[k, s - 2, :, cols(c)],
                    8, rzb.at[c, s - 2], at_z(sign),
                )

    def spread(src, c, sign, first, far):
        for d in far:
            to_rows = pl.ds(pl.multiple_of(((g + d) % GS) * 16, 16), 16)
            n = first + d
            send(src.at[to_rows, cols(c)], fin_in.at[n, :, cols(c)], 9, rf.at[c], at_zx(sign, d))

    def tables():
        await_all(meta.at[pl.ds(1, ZS - 1)], rm.at[0])

    def loaded():
        for ref, n in ((w_gu, 1), (w_d, 2), (residual, 3)):
            await_all(ref, sl.at[n])

    def finish(c):
        await_all(fin_in.at[:, :, cols(c)], rf.at[c])
        here, there = cols(c), cols(c, half)
        moe = fin[my_rows, here].astype(F32)
        for n in (1, 3, 5, 7, 9):
            moe = moe + fin_in[n, :, here].astype(F32)
        first, size = PIECES[c]
        at = pl.ds(pl.multiple_of(mine + first * 128, 128), size * 128)
        out[:, at] = (residual[:, here].astype(F32) + moe).astype(BF16)
        moe = fin_in[0, :, here].astype(F32)
        for n in (2, 4, 6, 8, 10):
            moe = moe + fin_in[n, :, here].astype(F32)
        at = pl.ds(pl.multiple_of(theirs + first * 128, 128), size * 128)
        out[:, at] = (residual[:, there].astype(F32) + moe).astype(BF16)

    steps = dict(
        table=table, tables=tables, weigh=weigh, z_event=z_event, select=select, y_event=y_event, loaded=loaded, x_event=x_event,
        project_own=project_own, project=project, activate=activate, down=down, down_own=down_own, xb_event=xb_event, yb_event=yb_event, finish=finish,
    )
    for step, *given in ORDER:
        steps[step](*given)
    five = rows.at[pl.ds(0, 5)]
    sizes = (fin_in, meta.at[pl.ds(0, ZS - 1)], five, y_out, other, gu_out, other, q_out, five, fin_in)
    for n, ref in enumerate(sizes):
        await_all(ref, sent.at[n])


def body(hidden_rows, routes, route_gain, gate_weight, up_weight, down_weight):
    hid = hidden_rows[0]
    n, width = hid.shape
    ff = gate_weight.shape[1]
    half = width // 2
    picked, gains = (jnp.transpose(v, (2, 0, 1)) for v in (routes, route_gain))
    total, n_c = ZS * SLAB, len(PIECES)
    vmem = pltpu.VMEM
    dma = pltpu.SemaphoreType.DMA
    any_spec = pl.BlockSpec(memory_space=pl.ANY)
    out = pl.pallas_call(
        kernel,
        out_shape=pltpu.VMEM((n, width), BF16),
        in_specs=[pl.BlockSpec(memory_space=pltpu.VMEM)] * 2 + [any_spec] * 4,
        out_specs=pl.BlockSpec(memory_space=pltpu.VMEM),
        scratch_shapes=[
            vmem((ZS, 16, 128), F32),
            vmem((ZS, SLAB, half), BF16),
            vmem((ZS, YS, CAPS, width), BF16),
            vmem((ZS, 3, CAPS, half), BF16),
            vmem((2 * ff, width), BF16),
            vmem((ff, width), BF16),
            vmem((ZS, YS * CAPS, SLAB), BF16),
            vmem((ZS, SLAB, YS * CAPS), BF16),
            vmem((total, 2 * ff), F32),
            vmem((total, 2 * ff), BF16),
            vmem((total, 2 * ff), BF16),
            vmem((total, ff), BF16),
            vmem((ZS, YS, CAPS, half), F32),
            vmem((ZS, YS, CAPS, half), BF16),
            vmem((ZS, YS, CAPS, half), BF16),
            vmem((ZS, 3, CAPS, half), BF16),
            vmem((ZS, YS, CAPS, half), BF16),
            vmem((2, 4, SLAB, half), BF16),
            vmem((2, 3, SLAB, half), BF16),
            vmem((SLAB, half), BF16),
            vmem((11, 16, half), BF16),
            vmem((n, width), BF16),
            dma((10,)), dma((n_c, 2)), dma((1,)), dma((n_c, 3)), dma((2, 5)), dma((5,)), dma((4,)),
            dma((n_c, 5)), dma((n_c, 5)), dma((n_c, 3)), dma((n_c,)), dma((4,)),
        ],
        compiler_params=pltpu.CompilerParams(
            collective_id=0, has_side_effects=True, vmem_limit_bytes=60 * 1024 * 1024
        ),
        name="routed_layer",
    )(picked, gains, hid, gate_weight[0], up_weight[0], down_weight[0])
    return out[None]


def solution(mesh):
    placed = (
        P("exp", "grp", "attn"),
        P("exp", None, None),
        P("exp", None, None),
        P("exp", "grp", "attn"),
        P("exp", "grp", "attn"),
        P("exp", "grp", "attn"),
    )
    return jax.shard_map(
        body, mesh=mesh, in_specs=placed, out_specs=P("exp", "grp", "attn"), check_vma=False
    )
```
